512 devices in a mesh: dom: 32 (over y, x, core), sub: 16 (over z).
Axes of the slice: x: 4, y: 4, z: 16, core: 2. Of those that a mesh axis runs over, the one named last changes fastest.
Arguments:
- state: float32 [5, 512, 65536], P(None, None, ('dom', 'sub')), may hold values from -1.5 to 7, as said below
- face_links: int32 [3, 3, 65536], P(None, None, ('dom', 'sub')), may hold values from 0 to 703, as said below
- send_from: int32 [512, 320], P(('dom', 'sub')), may hold values from 0 to 384, as said below
Outputs:
- update: float32 [5, 512, 65536], P(None, None, ('dom', 'sub'))
- section: float32 [5, 512, 65536], P(None, None, ('dom', 'sub'))
The draws below stay inside these ranges and needn't reach their ends.
Inputs may be any that keep to these rules, and one draw needn't show every extreme that they name: `state`: density and pressure are 0.5 or more at every node. face_links[0, k, g]: partner of element g's upper side in direction k, a lower side in direction k: a value below 384 is that lower side's flat index on the same device, a value p from 384 on is received slot p - 384. face_links[1, k, g]: for element g's lower side in direction k, below 384 the flat index of its upper side on the same device, else returned slot minus 3 * 128. face_links[2]: quarter turns, 0 to 3. Every side is in exactly one face. Slots of the blocks for odd dom offsets carry faces in direction 0, of even dom offsets direction 1, of sub offsets direction 2. Two devices share at most 32 faces each way, and in every draw some device shares exactly 32 each way with every neighbour. send_from[d, q] is the flat index of the lower side sent in slot q, or 384 for an empty slot; the first slots of each block are used. The lower side in slot q of block o of device d is the partner of the upper side that the device at offset o links to its slot q of block -o, and that device's slot q of block -o carries a lower side of it in turn.
All inputs are finite; a program needn't handle non-finite values.
Results may differ from the reference program's by a relative error of at most 0.0003.
Values sent between devices are 32-bit elements; how exact they have to be, the bound alone decides.
A program may use at most 128 MiB of HBM per device.

```python
import jax
import jax.numpy as jnp
import numpy as np
from jax import lax

NP = 8
NODES = 512
E_DEV = 128
CAP = 32
W_DOM = 4
SLOTS = 320
ELEMS = 65536
N_DOM = 32
N_SUB = 16


GAMMA = 1.4


def dom_offsets_drawn():
    return [offset for offset in range(-W_DOM, W_DOM + 1) if offset != 0]


def build_mesh(key):
    devices = N_DOM * N_SUB
    dom_key, sub_key, full_key, perm_key = jax.random.split(key, 4)
    dom_raw = jnp.triu(jax.random.randint(dom_key, (N_SUB, N_DOM, N_DOM), 1, CAP + 1), 1)
    dom_count = dom_raw + jnp.swapaxes(dom_raw, 1, 2)
    sub_raw = jnp.triu(jax.random.randint(sub_key, (N_DOM, N_SUB, N_SUB), 1, CAP + 1), 1)
    sub_count = sub_raw + jnp.swapaxes(sub_raw, 1, 2)
    full_dom = jax.random.randint(jax.random.fold_in(full_key, 1), (), 0, N_DOM)
    full_sub = jax.random.randint(jax.random.fold_in(full_key, 2), (), 0, N_SUB - 1)
    dom_count = dom_count.at[full_sub, full_dom, :].set(CAP).at[full_sub, :, full_dom].set(CAP)
    sub_count = sub_count.at[full_dom, full_sub, :].set(CAP).at[full_dom, :, full_sub].set(CAP)
    offsets = dom_offsets_drawn()
    block_dirs = jnp.array([0 if abs(offset) % 2 == 1 else 1 for offset in offsets] + [2, 2], jnp.int32)

    def tables(device, device_key):
        dom_index = device // N_SUB
        sub_index = device % N_SUB
        counts = []
        for offset in offsets:
            peer_index = dom_index + offset
            inside = (peer_index >= 0) & (peer_index < N_DOM)
            counts.append(jnp.where(inside, dom_count[sub_index, dom_index, jnp.clip(peer_index, 0, N_DOM - 1)], 0))
        for offset in (-1, 1):
            peer_index = sub_index + offset
            inside = (peer_index >= 0) & (peer_index < N_SUB)
            counts.append(jnp.where(inside, sub_count[dom_index, sub_index, jnp.clip(peer_index, 0, N_SUB - 1)], 0))
        counts = jnp.stack(counts)
        slots_valid = (jnp.arange(CAP, dtype=jnp.int32)[None, :] < counts[:, None]).reshape(-1)
        slot_dirs = jnp.repeat(block_dirs, CAP)
        slot_ids = jnp.arange(SLOTS, dtype=jnp.int32)
        rank_ids = jnp.arange(E_DEV, dtype=jnp.int32)
        send_table = jnp.full((SLOTS,), 3 * E_DEV, jnp.int32)
        partners = []
        sources = []
        for direction in range(3):
            upper_perm = jax.random.permutation(jax.random.fold_in(device_key, 2 * direction), E_DEV).astype(jnp.int32)
            lower_perm = jax.random.permutation(jax.random.fold_in(device_key, 2 * direction + 1), E_DEV).astype(jnp.int32)
            chosen = slots_valid & (slot_dirs == direction)
            slot_rank = jnp.cumsum(chosen.astype(jnp.int32)) - 1
            remote_total = jnp.sum(chosen.astype(jnp.int32))
            slot_of_rank = jnp.full((E_DEV,), SLOTS, jnp.int32).at[jnp.where(chosen, slot_rank, E_DEV)].set(slot_ids, mode='drop')
            remote = rank_ids < remote_total
            partner_by_rank = jnp.where(remote, 3 * E_DEV + slot_of_rank, direction * E_DEV + lower_perm)
            source_by_rank = jnp.where(remote, 3 * E_DEV + slot_of_rank, direction * E_DEV + upper_perm)
            partners.append(jnp.zeros((E_DEV,), jnp.int32).at[upper_perm].set(partner_by_rank))
            sources.append(jnp.zeros((E_DEV,), jnp.int32).at[lower_perm].set(source_by_rank))
            send_table = jnp.where(chosen, direction * E_DEV + lower_perm[jnp.clip(slot_rank, 0, E_DEV - 1)], send_table)
        quarter_turns = jax.random.randint(jax.random.fold_in(device_key, 7), (3, E_DEV), 0, 4)
        return (jnp.stack([jnp.stack(partners), jnp.stack(sources), quarter_turns]), send_table)
    device_keys = jax.random.split(perm_key, devices)
    link_table, send_table = jax.vmap(tables)(jnp.arange(devices, dtype=jnp.int32), device_keys)
    face_table = jnp.transpose(link_table, (1, 2, 0, 3)).reshape(3, 3, devices * E_DEV)
    return (face_table, send_table)


def draw_face_links(key, part):
    return build_mesh(key)[0]


def draw_send_from(key, part):
    return build_mesh(key)[1]


def draw_state(key, part):
    key = jax.random.fold_in(key, 11)
    first_key, second_key, third_key = jax.random.split(key, 3)
    field_shape = (NODES, ELEMS)
    density = jax.random.uniform(first_key, field_shape, jnp.float32, 0.7, 1.3)
    velocity = jax.random.uniform(second_key, (3,) + field_shape, jnp.float32, -0.4, 0.4)
    pressure = jax.random.uniform(third_key, field_shape, jnp.float32, 0.7, 1.3)
    momentum = density * velocity
    energy = pressure / (GAMMA - 1.0) + 0.5 * density * (velocity[0] * velocity[0] + velocity[1] * velocity[1] + velocity[2] * velocity[2])
    return jnp.concatenate([density[None], momentum, energy[None]], axis=0)


def setup_inputs(seed: int = 0) -> dict:
    keys = jax.random.split(jax.random.key(seed), 4)
    return {
        "state": draw_state(jax.random.fold_in(keys[3], 71), 0),
        "face_links": draw_face_links(jax.random.fold_in(keys[3], 71), 0),
        "send_from": draw_send_from(jax.random.fold_in(keys[3], 71), 0),
    }


GAMMA = 1.4
VISCOSITY = 0.02
CONDUCTION = VISCOSITY * GAMMA / ((GAMMA - 1.0) * 0.72)
PENALTY = 0.4
TIME_STEP = 0.02
SECTION_WEIGHT = 1432997174477.0 / 9575080441755.0

def lobatto(points):
    poly_order = points - 1
    abscissa = -np.cos(np.pi * np.arange(points) / poly_order)
    for sweep in range(60):
        before = abscissa * 0.0 + 1.0
        current = abscissa
        for degree in range(2, points):
            before, current = (current, ((2 * degree - 1) * abscissa * current - (degree - 1) * before) / degree)
        abscissa = abscissa - (abscissa * current - before) / (points * current)
    identity = np.eye(points)
    spacing = abscissa[:, None] - abscissa[None, :] + identity
    barycentric = 1.0 / np.prod(spacing, axis=1)
    matrix = barycentric[None, :] / barycentric[:, None] / spacing * (1.0 - identity)
    matrix = matrix - identity * np.sum(matrix, axis=1)[:, None]
    return (matrix, 2.0 / (poly_order * points))

def derivative(matrix, node_field, direction):
    einsum_forms = ('im,cmjle->cijle', 'jm,cimle->cijle', 'lm,cijme->cijle')
    return jnp.einsum(einsum_forms[direction], matrix, node_field, precision=lax.Precision.HIGHEST)

def face_of(node_field, direction, end_node):
    face_index = (slice(None),) * (direction + 1) + (end_node,)
    return node_field[face_index]

def add_face(node_field, direction, end_node, values):
    face_index = (slice(None),) * (direction + 1) + (end_node,)
    return node_field.at[face_index].add(values)

def lower_traces(state):
    node_cube = state.reshape(5, NP, NP, NP, -1)
    return jnp.concatenate([face_of(node_cube, direction, 0).reshape(5, NP * NP, -1) for direction in range(3)], axis=2)

def primitive(conserved):
    density = conserved[0]
    velocity = conserved[1:4] / density
    pressure = (GAMMA - 1.0) * (conserved[4] - 0.5 * (conserved[1] * velocity[0] + conserved[2] * velocity[1] + conserved[3] * velocity[2]))
    return (density, velocity, pressure)

def euler_flux(conserved, velocity, pressure, direction):
    normal_speed = velocity[direction]
    momentum = conserved[1:4] * normal_speed
    momentum = momentum.at[direction].add(pressure)
    return jnp.concatenate([conserved[1 + direction][None], momentum, ((conserved[4] + pressure) * normal_speed)[None]], axis=0)

def viscous_flux(velocity, gradients, direction):
    divergence = gradients[0, 0] + gradients[1, 1] + gradients[2, 2]
    stress = [VISCOSITY * (gradients[column, direction] + gradients[direction, column]) for column in range(3)]
    stress[direction] = stress[direction] - 2.0 / 3.0 * VISCOSITY * divergence
    heat_flux = velocity[0] * stress[0] + velocity[1] * stress[1] + velocity[2] * stress[2] + CONDUCTION * gradients[direction, 3]
    return jnp.stack([jnp.zeros_like(heat_flux)] + stress + [heat_flux], axis=0)

def orient(values, quarter_turns):
    node_grid = values.reshape(values.shape[0], NP, NP, -1)
    result = node_grid
    for quarter in range(1, 4):
        result = jnp.where(quarter_turns == quarter, jnp.rot90(node_grid, quarter, axes=(1, 2)), result)
    return result.reshape(values.shape)

def element_terms(state, slave_faces, matrix, end_weight):
    node_cube = state.reshape(5, NP, NP, NP, -1)
    elem_count = node_cube.shape[-1]
    density, velocity, pressure = primitive(node_cube)
    lifted = jnp.concatenate([velocity, (pressure / density)[None]], axis=0)
    slave_grid = slave_faces.reshape(5, NP, NP, 3, elem_count)
    slave_density, slave_velocity, slave_pressure = primitive(slave_grid)
    slave_lifted = jnp.concatenate([slave_velocity, (slave_pressure / slave_density)[None]], axis=0)
    gradients = []
    for direction in range(3):
        partial_grad = derivative(matrix, lifted, direction)
        lift_jump = (slave_lifted[:, :, :, direction] - face_of(lifted, direction, NP - 1)) / end_weight
        gradients.append(add_face(partial_grad, direction, NP - 1, lift_jump))
    gradients = jnp.stack(gradients)
    sound_speed = jnp.sqrt(GAMMA * pressure / density)
    slave_sound = jnp.sqrt(GAMMA * slave_pressure / slave_density)
    residual_rate = jnp.zeros_like(node_cube)
    master_flux = []
    lower_inner = []
    for direction in range(3):
        euler = euler_flux(node_cube, velocity, pressure, direction)
        viscous = viscous_flux(velocity, gradients, direction)
        total_flux = euler - viscous
        residual_rate = residual_rate - derivative(matrix, total_flux, direction)
        own_face = face_of(node_cube, direction, NP - 1)
        slave_state = slave_grid[:, :, :, direction]
        own_speed = jnp.abs(face_of(velocity, direction, NP - 1)[direction]) + face_of(sound_speed[None], direction, NP - 1)[0]
        other_speed = jnp.abs(slave_velocity[direction, :, :, direction]) + slave_sound[:, :, direction]
        wave_speed = jnp.maximum(own_speed, other_speed)
        other_euler = euler_flux(slave_state, slave_velocity[:, :, :, direction], slave_pressure[:, :, direction], direction)
        numeric = 0.5 * (face_of(euler, direction, NP - 1) + other_euler) + (0.5 * wave_speed + PENALTY) * (own_face - slave_state) - face_of(viscous, direction, NP - 1)
        residual_rate = add_face(residual_rate, direction, NP - 1, (face_of(total_flux, direction, NP - 1) - numeric) / end_weight)
        master_flux.append(numeric.reshape(5, NP * NP, elem_count))
        lower_inner.append(face_of(total_flux, direction, 0).reshape(5, NP * NP, elem_count))
    return (residual_rate, jnp.concatenate(master_flux, axis=2), jnp.concatenate(lower_inner, axis=2))

def finish(residual_rate, lower_flux, lower_inner, end_weight):
    elem_count = residual_rate.shape[-1]
    summed = lower_flux + lower_inner
    for direction in range(3):
        one_block = summed[:, :, direction * elem_count:(direction + 1) * elem_count].reshape(5, NP, NP, elem_count)
        residual_rate = add_face(residual_rate, direction, 0, -one_block / end_weight)
    return residual_rate.reshape(5, NP * NP * NP, elem_count)

def dom_offsets():
    return [offset for offset in range(-W_DOM, W_DOM + 1) if offset != 0]

def route(buffers):
    block_total = 2 * W_DOM + 2
    node_grid = buffers.reshape(N_DOM, N_SUB, 5, NP * NP, block_total, CAP)
    offsets = dom_offsets()
    pieces = [None] * block_total
    dom_rows = jnp.arange(N_DOM)
    for block_place, offset in enumerate(offsets):
        moved = jnp.roll(node_grid[:, :, :, :, block_place], offset, axis=0)
        inside = ((dom_rows - offset >= 0) & (dom_rows - offset < N_DOM))[:, None, None, None, None]
        pieces[len(offsets) - 1 - block_place] = jnp.where(inside, moved, 0.0)
    sub_rows = jnp.arange(N_SUB)
    for block_place, offset in enumerate((-1, 1)):
        moved = jnp.roll(node_grid[:, :, :, :, len(offsets) + block_place], offset, axis=1)
        inside = ((sub_rows - offset >= 0) & (sub_rows - offset < N_SUB))[None, :, None, None, None]
        pieces[len(offsets) + 1 - block_place] = jnp.where(inside, moved, 0.0)
    stacked = jnp.stack(pieces, axis=4)
    return stacked.reshape(N_DOM * N_SUB, 5, NP * NP, SLOTS)

def reference(state, face_links, send_from):
    devices = N_DOM * N_SUB
    matrix_table, end_weight = lobatto(NP)
    matrix = jnp.asarray(matrix_table, jnp.float32)
    by_device = jnp.moveaxis(state.reshape(5, NODES, devices, E_DEV), 2, 0)
    link_table = jnp.moveaxis(face_links.reshape(3, 3, devices, E_DEV), 2, 0).reshape(devices, 3, 3 * E_DEV)

    def outgoing_of(operands):
        device_state, send_table = operands
        lower = lower_traces(device_state)
        padded = jnp.concatenate([lower, jnp.zeros((5, NP * NP, 1), lower.dtype)], axis=2)
        return jnp.take(padded, send_table, axis=2)
    inbound = route(lax.map(outgoing_of, (by_device, send_from)))

    def slave_faces_of(device_state, links, received):
        lower = lower_traces(device_state)
        gathered = jnp.take(jnp.concatenate([lower, received], axis=2), links[0], axis=2)
        return orient(gathered, links[2])

    def master_side(operands):
        device_state, links, received = operands
        slave_faces = slave_faces_of(device_state, links, received)
        residual_rate, master_flux, lower_inner = element_terms(device_state, slave_faces, matrix, end_weight)
        slave_flux = -orient(master_flux, (4 - links[2]) % 4)
        return_slot = jnp.where(links[0] >= 3 * E_DEV, links[0] - 3 * E_DEV, SLOTS)
        returning = jnp.zeros((5, NP * NP, SLOTS), slave_flux.dtype).at[:, :, return_slot].set(slave_flux, mode='drop')
        return (slave_flux, returning)
    slave_fluxes, returning = lax.map(master_side, (by_device, link_table, inbound))
    returned = route(returning)

    def finish_side(operands):
        device_state, links, received, slave_flux, came_back = operands
        slave_faces = slave_faces_of(device_state, links, received)
        residual_rate, master_flux, lower_inner = element_terms(device_state, slave_faces, matrix, end_weight)
        lower_flux = jnp.take(jnp.concatenate([slave_flux, came_back], axis=2), links[1], axis=2)
        residual_rate = finish(residual_rate, lower_flux, lower_inner, end_weight)
        update = TIME_STEP * residual_rate
        return (update, device_state + SECTION_WEIGHT * update)
    updates, sections = lax.map(finish_side, (by_device, link_table, inbound, slave_fluxes, returned))
    update = jnp.moveaxis(updates, 0, 2).reshape(5, NODES, devices * E_DEV)
    section = jnp.moveaxis(sections, 0, 2).reshape(5, NODES, devices * E_DEV)
    return (update, section)
```

```python
import functools

import jax
import jax.numpy as jnp
import numpy as np
from jax import lax
from jax.experimental import pallas as pl
from jax.experimental.pallas import tpu as pltpu
from jax.sharding import PartitionSpec as P

NP = 8
LANES = 128
GAMMA = 1.4
VISCOSITY = 0.02
CONDUCTION = VISCOSITY * GAMMA / ((GAMMA - 1.0) * 0.72)
PENALTY = 0.4
TIME_STEP = 0.02
SECTION_WEIGHT = 1432997174477.0 / 9575080441755.0
OFFSETS = [("dom", o) for o in (-4, -3, -2, -1, 1, 2, 3, 4)] + [("sub", -1), ("sub", 1)]
MIRROR = [7, 6, 5, 4, 3, 2, 1, 0, 9, 8]
PLACES = [[1, 3, 4, 6], [0, 2, 5, 7], [8, 9]]


def lobatto(points):
    poly_order = points - 1
    abscissa = -np.cos(np.pi * np.arange(points) / poly_order)
    for sweep in range(60):
        before = abscissa * 0.0 + 1.0
        current = abscissa
        for degree in range(2, points):
            before, current = (
                current,
                ((2 * degree - 1) * abscissa * current - (degree - 1) * before) / degree,
            )
        abscissa = abscissa - (abscissa * current - before) / (points * current)
    identity = np.eye(points)
    spacing = abscissa[:, None] - abscissa[None, :] + identity
    barycentric = 1.0 / np.prod(spacing, axis=1)
    matrix = barycentric[None, :] / barycentric[:, None] / spacing * (1.0 - identity)
    matrix = matrix - identity * np.sum(matrix, axis=1)[:, None]
    return (matrix, 2.0 / (poly_order * points))


DMAT, W_END = lobatto(NP)
GRAD_MAT = VISCOSITY * DMAT
LIFT = VISCOSITY / W_END
FLUX_MAT = DMAT.copy()
FLUX_MAT[NP - 1, NP - 1] -= 1.0 / W_END
FLUX_MAT[0, 0] += 1.0 / W_END
FLUX_MAT = -TIME_STEP * FLUX_MAT
FACE_SCALE = TIME_STEP / W_END


def iota(axis):
    return lax.broadcasted_iota(jnp.int32, (NP, LANES), axis)


def lane_gather(x, index):
    return jnp.take_along_axis(x, index, axis=1, mode="promise_in_bounds")


def row_gather(x, index):
    return jnp.take_along_axis(x, index, axis=0, mode="promise_in_bounds")


def pencil(matrix, xs):
    even = [xs[m] + xs[7 - m] for m in range(4)]
    odd = [xs[m] - xs[7 - m] for m in range(4)]
    out = [None] * 8
    for i in range(4):
        a = b = None
        for m in range(4):
            ce = float(0.5 * (matrix[i, m] + matrix[i, 7 - m]))
            co = float(0.5 * (matrix[i, m] - matrix[i, 7 - m]))
            a = ce * even[m] if a is None else a + ce * even[m]
            b = co * odd[m] if b is None else b + co * odd[m]
        out[i] = a + b
        out[7 - i] = b - a
    return out


def roll_table(matrix):
    row = iota(0)
    table = []
    for r in range(NP):
        c = jnp.zeros((NP, LANES), jnp.float32)
        for l in range(NP):
            c = jnp.where(row == l, float(matrix[l, (l - r) % NP]), c)
        table.append(c)
    return table


def along_rows(table, x):
    acc = table[0] * x
    for r in range(1, NP):
        acc = acc + table[r] * pltpu.roll(x, r, 0)
    return acc


def tile(i, j):
    return pl.ds(pl.multiple_of(i * 64 + j * 8, 8), 8)


def face_rows(k, a, end):
    if k == 0:
        return pl.ds(pl.multiple_of(end * 64 + a * 8, 8), 8)
    if k == 1:
        return pl.ds(pl.multiple_of(a * 64 + end * 8, 8), 8)
    return pl.ds(a * 64 + end, 8, stride=8)


def grid_rows(a):
    return pl.ds(pl.multiple_of(a * 8, 8), 8)


def wide(row):
    return jnp.broadcast_to(row, (NP, LANES))


def select_groups(group, pieces):
    out = pieces[-1][1]
    for g, value in pieces[:-1]:
        out = jnp.where(group == g, value, out)
    return out


def primitive(u):
    inv = 1.0 / u[0]
    v = [u[1] * inv, u[2] * inv, u[3] * inv]
    p = (GAMMA - 1.0) * (u[4] - 0.5 * (u[1] * v[0] + u[2] * v[1] + u[3] * v[2]))
    return v, p, p * inv


def orient(load, store, turns, back):
    m = [load(grid_rows(a)) for a in range(NP)]
    t = [load(pl.ds(a, 8, stride=8)) for a in range(NP)]
    row = iota(0)
    one, three = (3, 1) if back else (1, 3)
    kept = (turns == 0) | (turns == one)
    index = jnp.where(kept, row, 7 - row)
    for a in range(NP):
        x = jnp.where(turns == 0, m[a], jnp.where(turns == one, t[7 - a], jnp.where(turns == 2, m[7 - a], t[a])))
        store(a, row_gather(x, index))


def kernel(n_dom, n_sub, state_ref, links_ref, send_ref, upd_out, sec_out,
           st, prim, grad, flux, upd, sec, low, pre, sl, mf, sf, send1, recv1, send2, recv2,
           in_sem, out_sem, send_sem, recv_sem):
    me = {"dom": lax.axis_index("dom"), "sub": lax.axis_index("sub")}
    size = {"dom": n_dom, "sub": n_sub}

    def device(place):
        axis, offset = OFFSETS[place]
        at = dict(me)
        at[axis] = lax.rem(me[axis] + offset + size[axis], size[axis])
        return (at["dom"], at["sub"])

    load_state = pltpu.make_async_copy(state_ref, st, in_sem)
    load_state.start()
    barrier = pltpu.get_barrier_semaphore()
    for place in range(10):
        pl.semaphore_signal(barrier, inc=1, device_id=device(place), device_id_type=pl.DeviceIdType.MESH)

    def remote(phase, place):
        src, dst = (send1, recv1) if phase == 0 else (send2, recv2)
        return pltpu.make_async_remote_copy(
            src_ref=src.at[place],
            dst_ref=dst.at[MIRROR[place]],
            send_sem=send_sem.at[phase, place],
            recv_sem=recv_sem.at[phase, MIRROR[place]],
            device_id=device(place),
            device_id_type=pl.DeviceIdType.MESH,
        )

    lane = iota(1)
    group = lane >> 5
    slot = lane & 31
    place_of = [
        jnp.where(group < 2, 2 * group + 1, 2 * group),
        jnp.where(group < 2, 2 * group, 2 * group + 1),
        8 + (group & 1),
    ]
    table = send_ref[...]
    t0, t1 = wide(table[:, 0:128]), wide(table[:, 128:256])
    t2 = wide(jnp.concatenate([table[:, 256:320], table[:, 256:320]], axis=1))
    send_index = []
    for k in range(2):
        at = (place_of[k] & 3) * 32 + slot
        send_index.append(jnp.where(group < 2, lane_gather(t0, at), lane_gather(t1, at)) & 127)
    send_index.append(t2 & 127)

    partner = [wide(links_ref[0, k : k + 1, :]) for k in range(3)]
    source = [wide(links_ref[1, k : k + 1, :]) for k in range(3)]
    turns = [wide(links_ref[2, k : k + 1, :]) for k in range(3)]

    def received_index(k, value):
        q = value - 384
        if k == 2:
            first = 1 - ((q >> 5) - 8)
        else:
            first = 3 - (q >> 6)
        return [(((first + j) & 3) * 32 + (q & 31)) for j in range(4)]

    return_index = []
    for k in range(3):
        column = jnp.broadcast_to(jnp.transpose(partner[k])[:, 0:1], (LANES, LANES))
        code = jnp.broadcast_to((384 + place_of[k] * 32 + slot)[0:1, :], (LANES, LANES))
        number = lax.broadcasted_iota(jnp.int32, (LANES, LANES), 0).astype(jnp.float32)
        found = jnp.sum(jnp.where(column == code, number, 0.0), axis=0, keepdims=True)
        return_index.append(wide(found.astype(jnp.int32)))

    def pack(k, get, index, buffer):
        rolled = [index] + [pltpu.roll(index, 32 * j, 1) for j in range(1, 4)]
        for r in range(10):
            u = [lane_gather(get(10 * j + r), rolled[j]) for j in range(4)]
            for b, place in enumerate(PLACES[k]):
                buffer[place, r * 8 : r * 8 + 8, :] = select_groups(group, [((b + j) % 4, u[j]) for j in range(4)])

    def unpack(k, r, buffer):
        v = [buffer[place, r * 8 : r * 8 + 8, :] for place in PLACES[k]]
        last = len(v) - 1
        return [select_groups(group, [((last - b + j) % 4, v[b]) for b in range(len(v))]) for j in range(4)]

    load_state.wait()
    for k in range(3):
        for c in range(5):
            for a in range(NP):
                low[k, c, a * 8 : a * 8 + 8, :] = st[c, face_rows(k, a, 0), :]
        pack(k, lambda n: low[k, n // 8, (n % 8) * 8 : (n % 8) * 8 + 8, :], send_index[k], send1)

    pl.semaphore_wait(barrier, 10)
    order = [0, 7, 1, 6, 2, 5, 3, 4, 8, 9]
    first = [remote(0, place) for place in order]
    for copy in first:
        copy.start()

    def prim_body(t, carry):
        rows = pl.ds(pl.multiple_of(t * 8, 8), 8)
        u = [st[c, rows, :] for c in range(5)]
        v, p, theta = primitive(u)
        for a in range(3):
            prim[a, rows, :] = v[a]
        prim[3, rows, :] = theta
        return carry

    lax.fori_loop(0, 64, prim_body, 0, unroll=4)

    grad_rows = roll_table(GRAD_MAT)

    def grad_body(s, carry):
        for a in range(4):
            xs = [prim[a, tile(i, s), :] for i in range(NP)]
            for i, y in enumerate(pencil(GRAD_MAT, xs)):
                grad[a, tile(i, s), :] = y
            xs = [prim[a, tile(s, j), :] for j in range(NP)]
            for j, y in enumerate(pencil(GRAD_MAT, xs)):
                grad[4 + a, tile(s, j), :] = y
            for j in range(NP):
                grad[8 + a, tile(s, j), :] = along_rows(grad_rows, xs[j])
        return carry

    lax.fori_loop(0, NP, grad_body, 0)

    for place in order:
        copy = remote(0, MIRROR[place])
        copy.wait_recv()
    for k in range(3):
        index = received_index(k, partner[k])
        own = partner[k] & 127
        local = partner[k] < 384
        for r in range(10):
            u = unpack(k, r, recv1)
            for j in range(4):
                n = 10 * j + r
                rows = slice((n % 8) * 8, (n % 8) * 8 + 8)
                pre[n // 8, rows, :] = jnp.where(
                    local, lane_gather(low[k, n // 8, rows, :], own), lane_gather(u[j], index[j])
                )
        for c in range(5):
            def keep(a, value, k=k, c=c):
                sl[k, c, a * 8 : a * 8 + 8, :] = value
            orient(lambda rows: pre[c, rows, :], keep, turns[k], False)

        def slave_body(a, carry, k=k):
            rows, at = grid_rows(a), face_rows(k, a, 7)
            s = [sl[k, c, rows, :] for c in range(5)]
            u = [st[c, at, :] for c in range(5)]
            vs, ps, ths = primitive(s)
            v = [prim[c, at, :] for c in range(3)]
            th = prim[3, at, :]
            p = th * u[0]
            for c in range(4):
                jump = (vs + [ths])[c] - (v + [th])[c]
                grad[4 * k + c, at, :] = grad[4 * k + c, at, :] + LIFT * jump
            speed = jnp.maximum(jnp.abs(v[k]) + jnp.sqrt(GAMMA * th), jnp.abs(vs[k]) + jnp.sqrt(GAMMA * ths))
            weight = 0.5 * speed + PENALTY
            e = [u[1 + k]] + [u[1 + j] * v[k] for j in range(3)] + [(u[4] + p) * v[k]]
            es = [s[1 + k]] + [s[1 + j] * vs[k] for j in range(3)] + [(s[4] + ps) * vs[k]]
            e[1 + k] = e[1 + k] + p
            es[1 + k] = es[1 + k] + ps
            for c in range(5):
                mf[k, c, rows, :] = 0.5 * (e[c] + es[c]) + weight * (u[c] - s[c])
            return carry

        lax.fori_loop(0, NP, slave_body, 0, unroll=2)

    def stress_heat(k, at, v):
        g = [[grad[4 * d + c, at, :] for c in range(3)] for d in range(3)]
        div = (2.0 / 3.0) * (g[0][0] + g[1][1] + g[2][2])
        stress = [g[k][j] + g[j][k] for j in range(3)]
        stress[k] = stress[k] - div
        heat = stress[0] * v[0] + stress[1] * v[1] + stress[2] * v[2]
        return stress, heat + (CONDUCTION / VISCOSITY) * grad[4 * k + 3, at, :]

    for k in (1, 0, 2):
        def viscous_body(a, carry, k=k):
            rows, at = grid_rows(a), face_rows(k, a, 7)
            v = [prim[c, at, :] for c in range(3)]
            stress, heat = stress_heat(k, at, v)
            for j in range(3):
                mf[k, 1 + j, rows, :] = mf[k, 1 + j, rows, :] - stress[j]
            mf[k, 4, rows, :] = mf[k, 4, rows, :] - heat
            return carry

        lax.fori_loop(0, NP, viscous_body, 0, unroll=2)
        for c in range(5):
            def keep(a, value, k=k, c=c):
                sf[k, c, a * 8 : a * 8 + 8, :] = value
            orient(lambda rows: mf[k, c, rows, :], keep, turns[k], True)
        pack(k, lambda n: sf[k, n // 8, (n % 8) * 8 : (n % 8) * 8 + 8, :], return_index[k], send2)
        for place in PLACES[k]:
            remote(1, place).start()

    def flux_body(t, carry):
        rows = pl.ds(pl.multiple_of(t * 8, 8), 8)
        u = [st[c, rows, :] for c in range(5)]
        v = [prim[c, rows, :] for c in range(3)]
        p = prim[3, rows, :] * u[0]
        g = [[grad[4 * d + c, rows, :] for c in range(4)] for d in range(3)]
        div = (2.0 / 3.0) * (g[0][0] + g[1][1] + g[2][2])
        stress = {}
        number = 0
        for a in range(3):
            for b in range(a, 3):
                stress[a, b] = stress[b, a] = g[a][b] + g[b][a] if a != b else 2.0 * g[a][a] - div
                total = u[1 + a] * v[b] - stress[a, b]
                flux[number, rows, :] = total + p if a == b else total
                number += 1
        enthalpy = u[4] + p
        for k in range(3):
            heat = stress[k, 0] * v[0] + stress[k, 1] * v[1] + stress[k, 2] * v[2]
            heat = heat + (CONDUCTION / VISCOSITY) * g[k][3]
            flux[6 + k, rows, :] = enthalpy * v[k] - heat
        return carry

    lax.fori_loop(0, 64, flux_body, 0, unroll=2)

    flux_rows = roll_table(FLUX_MAT)
    pairs = {(0, 0): 0, (0, 1): 1, (0, 2): 2, (1, 1): 3, (1, 2): 4, (2, 2): 5}

    def flux_of(k, c, rows):
        if c == 0:
            return st[1 + k, rows, :]
        if c == 4:
            return flux[6 + k, rows, :]
        return flux[pairs[min(k, c - 1), max(k, c - 1)], rows, :]

    def first_body(s, carry):
        for c in range(5):
            xs = [flux_of(0, c, tile(i, s)) for i in range(NP)]
            for i, y in enumerate(pencil(FLUX_MAT, xs)):
                upd[c, tile(i, s), :] = y
        return carry

    lax.fori_loop(0, NP, first_body, 0)

    def other_body(s, carry):
        for c in range(5):
            ys = pencil(FLUX_MAT, [flux_of(1, c, tile(s, j)) for j in range(NP)])
            for j in range(NP):
                rows = tile(s, j)
                upd[c, rows, :] = upd[c, rows, :] + ys[j] + along_rows(flux_rows, flux_of(2, c, rows))
        return carry

    lax.fori_loop(0, NP, other_body, 0)

    for k in range(3):
        for c in range(5):
            for a in range(NP):
                at = face_rows(k, a, 7)
                upd[c, at, :] = upd[c, at, :] - FACE_SCALE * mf[k, c, a * 8 : a * 8 + 8, :]

    for place in order:
        remote(1, MIRROR[place]).wait_recv()
    for k in range(3):
        index = received_index(k, source[k])
        own = source[k] & 127
        local = source[k] < 384
        for r in range(10):
            u = unpack(k, r, recv2)
            for j in range(4):
                n = 10 * j + r
                c, a = n // 8, n % 8
                value = jnp.where(
                    local, lane_gather(sf[k, c, a * 8 : a * 8 + 8, :], own), lane_gather(u[j], index[j])
                )
                at = face_rows(k, a, 0)
                upd[c, at, :] = upd[c, at, :] + FACE_SCALE * value

    def section_body(t, carry):
        rows = pl.ds(pl.multiple_of(t * 8, 8), 8)
        for c in range(5):
            sec[c, rows, :] = st[c, rows, :] + SECTION_WEIGHT * upd[c, rows, :]
        return carry

    store_upd = pltpu.make_async_copy(upd, upd_out, out_sem.at[0])
    store_upd.start()
    lax.fori_loop(0, 64, section_body, 0, unroll=4)
    store_sec = pltpu.make_async_copy(sec, sec_out, out_sem.at[1])
    store_sec.start()
    for phase in range(2):
        for place in order:
            remote(phase, place).wait_send()
    store_upd.wait()
    store_sec.wait()


def per_device(n_dom, n_sub, state, face_links, send_from):
    whole = pltpu.VMEM
    f32 = jnp.float32
    field = (512, LANES)
    return pl.pallas_call(
        functools.partial(kernel, n_dom, n_sub),
        out_shape=(jax.ShapeDtypeStruct(state.shape, f32), jax.ShapeDtypeStruct(state.shape, f32)),
        in_specs=[
            pl.BlockSpec(memory_space=pl.ANY),
            pl.BlockSpec(memory_space=whole),
            pl.BlockSpec(memory_space=whole),
        ],
        out_specs=(pl.BlockSpec(memory_space=pl.ANY), pl.BlockSpec(memory_space=pl.ANY)),
        scratch_shapes=[
            whole((5,) + field, f32),
            whole((4,) + field, f32),
            whole((12,) + field, f32),
            whole((9,) + field, f32),
            whole((5,) + field, f32),
            whole((5,) + field, f32),
            whole((3, 5, 64, LANES), f32),
            whole((5, 64, LANES), f32),
            whole((3, 5, 64, LANES), f32),
            whole((3, 5, 64, LANES), f32),
            whole((3, 5, 64, LANES), f32),
            whole((10, 80, LANES), f32),
            whole((10, 80, LANES), f32),
            whole((10, 80, LANES), f32),
            whole((10, 80, LANES), f32),
            pltpu.SemaphoreType.DMA,
            pltpu.SemaphoreType.DMA((2,)),
            pltpu.SemaphoreType.DMA((2, 10)),
            pltpu.SemaphoreType.DMA((2, 10)),
        ],
        compiler_params=pltpu.CompilerParams(
            collective_id=0, has_side_effects=True, vmem_limit_bytes=48 * 1024 * 1024
        ),
        name="section",
    )(state, face_links, send_from)


def solution(mesh):
    in_specs = (
        P(None, None, ("dom", "sub")),
        P(None, None, ("dom", "sub")),
        P(("dom", "sub"), None),
    )
    out_specs = (P(None, None, ("dom", "sub")), P(None, None, ("dom", "sub")))
    return jax.shard_map(
        functools.partial(per_device, mesh.shape["dom"], mesh.shape["sub"]),
        mesh=mesh, in_specs=in_specs, out_specs=out_specs, check_vma=False
    )
```

```python
import functools

import jax
import jax.numpy as jnp
import numpy as np
from jax import lax
from jax.experimental import pallas as pl
from jax.experimental.pallas import tpu as pltpu
from jax.sharding import PartitionSpec as P

NP = 8
LANES = 128
GAMMA = 1.4
VISCOSITY = 0.02
CONDUCTION = VISCOSITY * GAMMA / ((GAMMA - 1.0) * 0.72)
PENALTY = 0.4
TIME_STEP = 0.02
SECTION_WEIGHT = 1432997174477.0 / 9575080441755.0
OFFSETS = [("dom", o) for o in (-4, -3, -2, -1, 1, 2, 3, 4)] + [("sub", -1), ("sub", 1)]
MIRROR = [7, 6, 5, 4, 3, 2, 1, 0, 9, 8]
PLACES = [[1, 3, 4, 6], [0, 2, 5, 7], [8, 9]]


def lobatto(points):
    poly_order = points - 1
    abscissa = -np.cos(np.pi * np.arange(points) / poly_order)
    for sweep in range(60):
        before = abscissa * 0.0 + 1.0
        current = abscissa
        for degree in range(2, points):
            before, current = (
                current,
                ((2 * degree - 1) * abscissa * current - (degree - 1) * before) / degree,
            )
        abscissa = abscissa - (abscissa * current - before) / (points * current)
    identity = np.eye(points)
    spacing = abscissa[:, None] - abscissa[None, :] + identity
    barycentric = 1.0 / np.prod(spacing, axis=1)
    matrix = barycentric[None, :] / barycentric[:, None] / spacing * (1.0 - identity)
    matrix = matrix - identity * np.sum(matrix, axis=1)[:, None]
    return (matrix, 2.0 / (poly_order * points))


DMAT, W_END = lobatto(NP)
GRAD_MAT = VISCOSITY * DMAT
LIFT = VISCOSITY / W_END
FLUX_MAT = DMAT.copy()
FLUX_MAT[NP - 1, NP - 1] -= 1.0 / W_END
FLUX_MAT[0, 0] += 1.0 / W_END
FLUX_MAT = -TIME_STEP * FLUX_MAT
FACE_SCALE = TIME_STEP / W_END


def iota(axis):
    return lax.broadcasted_iota(jnp.int32, (NP, LANES), axis)


def lane_gather(x, index):
    return jnp.take_along_axis(x, index, axis=1, mode="promise_in_bounds")


def row_gather(x, index):
    return jnp.take_along_axis(x, index, axis=0, mode="promise_in_bounds")


def pencil(matrix, xs):
    even = [xs[m] + xs[7 - m] for m in range(4)]
    odd = [xs[m] - xs[7 - m] for m in range(4)]
    out = [None] * 8
    for i in range(4):
        a = b = None
        for m in range(4):
            ce = float(0.5 * (matrix[i, m] + matrix[i, 7 - m]))
            co = float(0.5 * (matrix[i, m] - matrix[i, 7 - m]))
            a = ce * even[m] if a is None else a + ce * even[m]
            b = co * odd[m] if b is None else b + co * odd[m]
        out[i] = a + b
        out[7 - i] = b - a
    return out


def roll_table(matrix):
    row = iota(0)
    table = []
    for r in range(NP):
        c = jnp.zeros((NP, LANES), jnp.float32)
        for l in range(NP):
            c = jnp.where(row == l, float(matrix[l, (l - r) % NP]), c)
        table.append(c)
    return table


def along_rows(table, x):
    acc = table[0] * x
    for r in range(1, NP):
        acc = acc + table[r] * pltpu.roll(x, r, 0)
    return acc


def tile(i, j):
    return pl.ds(pl.multiple_of(i * 64 + j * 8, 8), 8)


def face_rows(k, a, end):
    if k == 0:
        return pl.ds(pl.multiple_of(end * 64 + a * 8, 8), 8)
    if k == 1:
        return pl.ds(pl.multiple_of(a * 64 + end * 8, 8), 8)
    return pl.ds(a * 64 + end, 8, stride=8)


def grid_rows(a):
    return pl.ds(pl.multiple_of(a * 8, 8), 8)


def wide(row):
    return jnp.broadcast_to(row, (NP, LANES))


def select_groups(group, pieces):
    out = pieces[-1][1]
    for g, value in pieces[:-1]:
        out = jnp.where(group == g, value, out)
    return out


def primitive(u):
    inv = 1.0 / u[0]
    v = [u[1] * inv, u[2] * inv, u[3] * inv]
    p = (GAMMA - 1.0) * (u[4] - 0.5 * (u[1] * v[0] + u[2] * v[1] + u[3] * v[2]))
    return v, p, p * inv


def orient(load, store, turns, back):
    m = [load(grid_rows(a)) for a in range(NP)]
    t = [load(pl.ds(a, 8, stride=8)) for a in range(NP)]
    row = iota(0)
    one, three = (3, 1) if back else (1, 3)
    kept = (turns == 0) | (turns == one)
    index = jnp.where(kept, row, 7 - row)
    for a in range(NP):
        x = jnp.where(turns == 0, m[a], jnp.where(turns == one, t[7 - a], jnp.where(turns == 2, m[7 - a], t[a])))
        store(a, row_gather(x, index))


def kernel(n_dom, n_sub, state_hbm, links_hbm, send_hbm, upd, st,
           links_ref, send_ref, prim, grad, flux, low, pre, sl, mf, sf, send1, recv1, send2, recv2,
           in_sem, send_sem, recv_sem):
    me = {"dom": lax.axis_index("dom"), "sub": lax.axis_index("sub")}
    size = {"dom": n_dom, "sub": n_sub}

    def device(place):
        axis, offset = OFFSETS[place]
        at = dict(me)
        at[axis] = lax.rem(me[axis] + offset + size[axis], size[axis])
        return (at["dom"], at["sub"])

    loads = [pltpu.make_async_copy(state_hbm.at[c], st.at[c], in_sem.at[c]) for c in range(5)]
    loads.append(pltpu.make_async_copy(links_hbm, links_ref, in_sem.at[5]))
    loads.append(pltpu.make_async_copy(send_hbm, send_ref, in_sem.at[6]))
    barrier = pltpu.get_barrier_semaphore()
    for place in range(10):
        pl.semaphore_signal(barrier, inc=1, device_id=device(place), device_id_type=pl.DeviceIdType.MESH)

    for load in loads[::-1]:
        load.start()

    def remote(phase, place):
        src, dst = (send1, recv1) if phase == 0 else (send2, recv2)
        return pltpu.make_async_remote_copy(
            src_ref=src.at[place],
            dst_ref=dst.at[MIRROR[place]],
            send_sem=send_sem.at[phase, place],
            recv_sem=recv_sem.at[phase, MIRROR[place]],
            device_id=device(place),
            device_id_type=pl.DeviceIdType.MESH,
        )

    loads[6].wait()
    loads[5].wait()
    lane = iota(1)
    group = lane >> 5
    slot = lane & 31
    place_of = [
        jnp.where(group < 2, 2 * group + 1, 2 * group),
        jnp.where(group < 2, 2 * group, 2 * group + 1),
        8 + (group & 1),
    ]
    table = send_ref[...]
    t0, t1 = wide(table[:, 0:128]), wide(table[:, 128:256])
    t2 = wide(jnp.concatenate([table[:, 256:320], table[:, 256:320]], axis=1))
    send_index = []
    for k in range(2):
        at = (place_of[k] & 3) * 32 + slot
        send_index.append(jnp.where(group < 2, lane_gather(t0, at), lane_gather(t1, at)) & 127)
    send_index.append(t2 & 127)

    partner = [wide(links_ref[0, k : k + 1, :]) for k in range(3)]
    source = [wide(links_ref[1, k : k + 1, :]) for k in range(3)]
    turns = [wide(links_ref[2, k : k + 1, :]) for k in range(3)]

    def received_index(k, value):
        q = value - 384
        if k == 2:
            first = 1 - ((q >> 5) - 8)
        else:
            first = 3 - (q >> 6)
        return [(((first + j) & 3) * 32 + (q & 31)) for j in range(4)]

    return_index = []
    for k in range(3):
        column = jnp.broadcast_to(jnp.transpose(partner[k])[:, 0:1], (LANES, LANES))
        code = jnp.broadcast_to((384 + place_of[k] * 32 + slot)[0:1, :], (LANES, LANES))
        number = lax.broadcasted_iota(jnp.int32, (LANES, LANES), 0).astype(jnp.float32)
        found = jnp.sum(jnp.where(column == code, number, 0.0), axis=0, keepdims=True)
        return_index.append(wide(found.astype(jnp.int32)))

    def pack(k, get, index, buffer):
        rolled = [index] + [pltpu.roll(index, 32 * j, 1) for j in range(1, 4)]
        for r in range(10):
            u = [lane_gather(get(4 * r + j), rolled[j]) for j in range(4)]
            for b, place in enumerate(PLACES[k]):
                buffer[place, r * 8 : r * 8 + 8, :] = select_groups(group, [((b + j) % 4, u[j]) for j in range(4)])

    def unpack(k, r, buffer):
        v = [buffer[place, r * 8 : r * 8 + 8, :] for place in PLACES[k]]
        last = len(v) - 1
        return [select_groups(group, [((last - b + j) % 4, v[b]) for b in range(len(v))]) for j in range(4)]

    for c in range(5):
        loads[c].wait()
    for k in range(3):
        for c in range(5):
            for a in range(NP):
                low[k, c, a * 8 : a * 8 + 8, :] = st[c, face_rows(k, a, 0), :]
        pack(k, lambda n: low[k, n // 8, (n % 8) * 8 : (n % 8) * 8 + 8, :], send_index[k], send1)

    pl.semaphore_wait(barrier, 10)
    order = [0, 7, 1, 6, 2, 5, 3, 4, 8, 9]
    first = [remote(0, place) for place in order]
    for copy in first:
        copy.start()

    def prim_body(t, carry):
        rows = pl.ds(pl.multiple_of(t * 8, 8), 8)
        u = [st[c, rows, :] for c in range(5)]
        v, p, theta = primitive(u)
        for a in range(3):
            prim[a, rows, :] = v[a]
        prim[3, rows, :] = theta
        return carry

    lax.fori_loop(0, 64, prim_body, 0, unroll=4)

    grad_rows = roll_table(GRAD_MAT)

    def grad_body(s, carry):
        for a in range(4):
            xs = [prim[a, tile(i, s), :] for i in range(NP)]
            for i, y in enumerate(pencil(GRAD_MAT, xs)):
                grad[a, tile(i, s), :] = y
            xs = [prim[a, tile(s, j), :] for j in range(NP)]
            for j, y in enumerate(pencil(GRAD_MAT, xs)):
                grad[4 + a, tile(s, j), :] = y
            for j in range(NP):
                grad[8 + a, tile(s, j), :] = along_rows(grad_rows, xs[j])
        return carry

    lax.fori_loop(0, NP, grad_body, 0)

    for place in order:
        copy = remote(0, MIRROR[place])
        copy.wait_recv()
    for k in range(3):
        index = received_index(k, partner[k])
        own = partner[k] & 127
        local = partner[k] < 384
        for r in range(10):
            u = unpack(k, r, recv1)
            for j in range(4):
                n = 4 * r + j
                rows = slice((n % 8) * 8, (n % 8) * 8 + 8)
                pre[n // 8, rows, :] = jnp.where(
                    local, lane_gather(low[k, n // 8, rows, :], own), lane_gather(u[j], index[j])
                )
        for c in range(5):
            def keep(a, value, k=k, c=c):
                sl[k, c, a * 8 : a * 8 + 8, :] = value
            orient(lambda rows: pre[c, rows, :], keep, turns[k], False)

        def slave_body(a, carry, k=k):
            rows, at = grid_rows(a), face_rows(k, a, 7)
            s = [sl[k, c, rows, :] for c in range(5)]
            u = [st[c, at, :] for c in range(5)]
            vs, ps, ths = primitive(s)
            v = [prim[c, at, :] for c in range(3)]
            th = prim[3, at, :]
            p = th * u[0]
            for c in range(4):
                jump = (vs + [ths])[c] - (v + [th])[c]
                grad[4 * k + c, at, :] = grad[4 * k + c, at, :] + LIFT * jump
            speed = jnp.maximum(jnp.abs(v[k]) + jnp.sqrt(GAMMA * th), jnp.abs(vs[k]) + jnp.sqrt(GAMMA * ths))
            weight = 0.5 * speed + PENALTY
            e = [u[1 + k]] + [u[1 + j] * v[k] for j in range(3)] + [(u[4] + p) * v[k]]
            es = [s[1 + k]] + [s[1 + j] * vs[k] for j in range(3)] + [(s[4] + ps) * vs[k]]
            e[1 + k] = e[1 + k] + p
            es[1 + k] = es[1 + k] + ps
            for c in range(5):
                mf[k, c, rows, :] = 0.5 * (e[c] + es[c]) + weight * (u[c] - s[c])
            return carry

        lax.fori_loop(0, NP, slave_body, 0, unroll=2)

    def stress_heat(k, at, v):
        g = [[grad[4 * d + c, at, :] for c in range(3)] for d in range(3)]
        div = (2.0 / 3.0) * (g[0][0] + g[1][1] + g[2][2])
        stress = [g[k][j] + g[j][k] for j in range(3)]
        stress[k] = stress[k] - div
        heat = stress[0] * v[0] + stress[1] * v[1] + stress[2] * v[2]
        return stress, heat + (CONDUCTION / VISCOSITY) * grad[4 * k + 3, at, :]

    for k in (1, 0, 2):
        def viscous_body(a, carry, k=k):
            rows, at = grid_rows(a), face_rows(k, a, 7)
            v = [prim[c, at, :] for c in range(3)]
            stress, heat = stress_heat(k, at, v)
            for j in range(3):
                mf[k, 1 + j, rows, :] = mf[k, 1 + j, rows, :] - stress[j]
            mf[k, 4, rows, :] = mf[k, 4, rows, :] - heat
            return carry

        lax.fori_loop(0, NP, viscous_body, 0, unroll=2)
        for c in range(5):
            def keep(a, value, k=k, c=c):
                sf[k, c, a * 8 : a * 8 + 8, :] = value
            orient(lambda rows: mf[k, c, rows, :], keep, turns[k], True)
        pack(k, lambda n: sf[k, n // 8, (n % 8) * 8 : (n % 8) * 8 + 8, :], return_index[k], send2)
        for place in PLACES[k]:
            remote(1, place).start()

    def flux_body(t, carry):
        rows = pl.ds(pl.multiple_of(t * 8, 8), 8)
        u = [st[c, rows, :] for c in range(5)]
        v = [prim[c, rows, :] for c in range(3)]
        p = prim[3, rows, :] * u[0]
        g = [[grad[4 * d + c, rows, :] for c in range(4)] for d in range(3)]
        div = (2.0 / 3.0) * (g[0][0] + g[1][1] + g[2][2])
        stress = {}
        number = 0
        for a in range(3):
            for b in range(a, 3):
                stress[a, b] = stress[b, a] = g[a][b] + g[b][a] if a != b else 2.0 * g[a][a] - div
                total = u[1 + a] * v[b] - stress[a, b]
                flux[number, rows, :] = total + p if a == b else total
                number += 1
        enthalpy = u[4] + p
        for k in range(3):
            heat = stress[k, 0] * v[0] + stress[k, 1] * v[1] + stress[k, 2] * v[2]
            heat = heat + (CONDUCTION / VISCOSITY) * g[k][3]
            flux[6 + k, rows, :] = enthalpy * v[k] - heat
        return carry

    lax.fori_loop(0, 64, flux_body, 0, unroll=2)

    flux_rows = roll_table(FLUX_MAT)
    pairs = {(0, 0): 0, (0, 1): 1, (0, 2): 2, (1, 1): 3, (1, 2): 4, (2, 2): 5}

    def flux_of(k, c, rows):
        if c == 0:
            return st[1 + k, rows, :]
        if c == 4:
            return flux[6 + k, rows, :]
        return flux[pairs[min(k, c - 1), max(k, c - 1)], rows, :]

    def first_body(s, carry):
        for c in range(5):
            xs = [flux_of(0, c, tile(i, s)) for i in range(NP)]
            for i, y in enumerate(pencil(FLUX_MAT, xs)):
                upd[c, tile(i, s), :] = y
        return carry

    lax.fori_loop(0, NP, first_body, 0)

    def other_body(s, carry):
        for c in range(5):
            ys = pencil(FLUX_MAT, [flux_of(1, c, tile(s, j)) for j in range(NP)])
            for j in range(NP):
                rows = tile(s, j)
                upd[c, rows, :] = upd[c, rows, :] + ys[j] + along_rows(flux_rows, flux_of(2, c, rows))
        return carry

    lax.fori_loop(0, NP, other_body, 0)

    for k in range(3):
        for c in range(5):
            for a in range(NP):
                at = face_rows(k, a, 7)
                upd[c, at, :] = upd[c, at, :] - FACE_SCALE * mf[k, c, a * 8 : a * 8 + 8, :]

    for place in order:
        remote(1, MIRROR[place]).wait_recv()
    for k in range(3):
        index = received_index(k, source[k])
        own = source[k] & 127
        local = source[k] < 384
        for r in range(10):
            u = unpack(k, r, recv2)
            for j in range(4):
                n = 4 * r + j
                c, a = n // 8, n % 8
                value = jnp.where(
                    local, lane_gather(sf[k, c, a * 8 : a * 8 + 8, :], own), lane_gather(u[j], index[j])
                )
                at = face_rows(k, a, 0)
                upd[c, at, :] = upd[c, at, :] + FACE_SCALE * value

    for phase in range(2):
        for place in order:
            remote(phase, place).wait_send()


def writer(upd, st, upd_out, sec_out, sec, sem):
    copies = []
    for c in range(5):
        copies.append(pltpu.make_async_copy(upd.at[c], upd_out.at[c], sem.at[0, c]))
        copies[-1].start()
    for c in range(5):
        sec[c] = st[c] + SECTION_WEIGHT * upd[c]
        copies.append(pltpu.make_async_copy(sec.at[c], sec_out.at[c], sem.at[1, c]))
        copies[-1].start()
    for copy in copies:
        copy.wait()


def per_device(n_dom, n_sub, state, face_links, send_from):
    whole = pltpu.VMEM
    f32 = jnp.float32
    field = (512, LANES)
    hbm = pl.BlockSpec(memory_space=pltpu.HBM)
    inside = pl.BlockSpec(memory_space=whole)
    like = jax.ShapeDtypeStruct(state.shape, f32)
    state, face_links, send_from = [
        pltpu.with_memory_space_constraint(x, pltpu.HBM) for x in (state, face_links, send_from)
    ]
    upd, st = pl.pallas_call(
        functools.partial(kernel, n_dom, n_sub),
        out_shape=(like, like),
        in_specs=[hbm, hbm, hbm],
        out_specs=(inside, inside),
        scratch_shapes=[
            whole(face_links.shape, jnp.int32),
            whole(send_from.shape, jnp.int32),
            whole((4,) + field, f32),
            whole((12,) + field, f32),
            whole((9,) + field, f32),
            whole((3, 5, 64, LANES), f32),
            whole((5, 64, LANES), f32),
            whole((3, 5, 64, LANES), f32),
            whole((3, 5, 64, LANES), f32),
            whole((3, 5, 64, LANES), f32),
            whole((10, 80, LANES), f32),
            whole((10, 80, LANES), f32),
            whole((10, 80, LANES), f32),
            whole((10, 80, LANES), f32),
            pltpu.SemaphoreType.DMA((7,)),
            pltpu.SemaphoreType.DMA((2, 10)),
            pltpu.SemaphoreType.DMA((2, 10)),
        ],
        compiler_params=pltpu.CompilerParams(
            collective_id=0, has_side_effects=True, vmem_limit_bytes=40 * 1024 * 1024
        ),
        name="rate",
    )(state, face_links, send_from)
    return pl.pallas_call(
        writer,
        out_shape=(like, like),
        in_specs=[inside, inside],
        out_specs=(hbm, hbm),
        scratch_shapes=[whole((5,) + field, f32), pltpu.SemaphoreType.DMA((2, 5))],
        compiler_params=pltpu.CompilerParams(vmem_limit_bytes=16 * 1024 * 1024),
        name="section",
    )(upd, st)


def solution(mesh):
    in_specs = (
        P(None, None, ("dom", "sub")),
        P(None, None, ("dom", "sub")),
        P(("dom", "sub"), None),
    )
    out_specs = (P(None, None, ("dom", "sub")), P(None, None, ("dom", "sub")))
    return jax.shard_map(
        functools.partial(per_device, mesh.shape["dom"], mesh.shape["sub"]),
        mesh=mesh, in_specs=in_specs, out_specs=out_specs, check_vma=False
    )
```

```python
import functools

import jax
import jax.numpy as jnp
import numpy as np
from jax import lax
from jax.experimental import pallas as pl
from jax.experimental.pallas import tpu as pltpu
from jax.sharding import PartitionSpec as P

NP = 8
LANES = 128
GAMMA = 1.4
VISCOSITY = 0.02
CONDUCTION = VISCOSITY * GAMMA / ((GAMMA - 1.0) * 0.72)
PENALTY = 0.4
TIME_STEP = 0.02
SECTION_WEIGHT = 1432997174477.0 / 9575080441755.0
OFFSETS = [("dom", o) for o in (-4, -3, -2, -1, 1, 2, 3, 4)] + [("sub", -1), ("sub", 1)]
MIRROR = [7, 6, 5, 4, 3, 2, 1, 0, 9, 8]
PLACES = [[1, 3, 4, 6], [0, 2, 5, 7], [8, 9]]


def lobatto(points):
    poly_order = points - 1
    abscissa = -np.cos(np.pi * np.arange(points) / poly_order)
    for sweep in range(60):
        before = abscissa * 0.0 + 1.0
        current = abscissa
        for degree in range(2, points):
            before, current = (
                current,
                ((2 * degree - 1) * abscissa * current - (degree - 1) * before) / degree,
            )
        abscissa = abscissa - (abscissa * current - before) / (points * current)
    identity = np.eye(points)
    spacing = abscissa[:, None] - abscissa[None, :] + identity
    barycentric = 1.0 / np.prod(spacing, axis=1)
    matrix = barycentric[None, :] / barycentric[:, None] / spacing * (1.0 - identity)
    matrix = matrix - identity * np.sum(matrix, axis=1)[:, None]
    return (matrix, 2.0 / (poly_order * points))


DMAT, W_END = lobatto(NP)
GRAD_MAT = VISCOSITY * DMAT
LIFT = VISCOSITY / W_END
FLUX_MAT = DMAT.copy()
FLUX_MAT[NP - 1, NP - 1] -= 1.0 / W_END
FLUX_MAT[0, 0] += 1.0 / W_END
FLUX_MAT = -TIME_STEP * FLUX_MAT
FACE_SCALE = TIME_STEP / W_END


def iota(axis):
    return lax.broadcasted_iota(jnp.int32, (NP, LANES), axis)


def lane_gather(x, index):
    return jnp.take_along_axis(x, index, axis=1, mode="promise_in_bounds")


def row_gather(x, index):
    return jnp.take_along_axis(x, index, axis=0, mode="promise_in_bounds")


def pencil(matrix, xs):
    even = [xs[m] + xs[7 - m] for m in range(4)]
    odd = [xs[m] - xs[7 - m] for m in range(4)]
    out = [None] * 8
    for i in range(4):
        a = b = None
        for m in range(4):
            ce = float(0.5 * (matrix[i, m] + matrix[i, 7 - m]))
            co = float(0.5 * (matrix[i, m] - matrix[i, 7 - m]))
            a = ce * even[m] if a is None else a + ce * even[m]
            b = co * odd[m] if b is None else b + co * odd[m]
        out[i] = a + b
        out[7 - i] = b - a
    return out


def roll_table(matrix):
    row = iota(0)
    table = []
    for r in range(NP):
        c = jnp.zeros((NP, LANES), jnp.float32)
        for l in range(NP):
            c = jnp.where(row == l, float(matrix[l, (l - r) % NP]), c)
        table.append(c)
    return table


def along_rows(table, x):
    acc = table[0] * x
    for r in range(1, NP):
        acc = acc + table[r] * pltpu.roll(x, r, 0)
    return acc


def tile(i, j):
    return pl.ds(pl.multiple_of(i * 64 + j * 8, 8), 8)


def face_rows(k, a, end):
    if k == 0:
        return pl.ds(pl.multiple_of(end * 64 + a * 8, 8), 8)
    if k == 1:
        return pl.ds(pl.multiple_of(a * 64 + end * 8, 8), 8)
    return pl.ds(a * 64 + end, 8, stride=8)


def grid_rows(a):
    return pl.ds(pl.multiple_of(a * 8, 8), 8)


def wide(row):
    return jnp.broadcast_to(row, (NP, LANES))


def select_groups(group, pieces):
    out = pieces[-1][1]
    for g, value in pieces[:-1]:
        out = jnp.where(group == g, value, out)
    return out


def primitive(u):
    inv = 1.0 / u[0]
    v = [u[1] * inv, u[2] * inv, u[3] * inv]
    p = (GAMMA - 1.0) * (u[4] - 0.5 * (u[1] * v[0] + u[2] * v[1] + u[3] * v[2]))
    return v, p, p * inv


def orient(load, store, turns, back):
    m = [load(grid_rows(a)) for a in range(NP)]
    t = [load(pl.ds(a, 8, stride=8)) for a in range(NP)]
    row = iota(0)
    one, three = (3, 1) if back else (1, 3)
    kept = (turns == 0) | (turns == one)
    index = jnp.where(kept, row, 7 - row)
    for a in range(NP):
        x = jnp.where(turns == 0, m[a], jnp.where(turns == one, t[7 - a], jnp.where(turns == 2, m[7 - a], t[a])))
        store(a, row_gather(x, index))


def kernel(n_dom, n_sub, state_hbm, links_hbm, send_hbm, upd, st,
           links_ref, send_ref, prim, grad, flux, low, pre, sl, mf, sf, send1, recv1, send2, recv2,
           in_sem, send_sem, recv_sem):
    me = {"dom": lax.axis_index("dom"), "sub": lax.axis_index("sub")}
    size = {"dom": n_dom, "sub": n_sub}

    def device(place):
        axis, offset = OFFSETS[place]
        at = dict(me)
        at[axis] = lax.rem(me[axis] + offset + size[axis], size[axis])
        return (at["dom"], at["sub"])

    def exists(place):
        axis, offset = OFFSETS[place]
        return (me[axis] + offset >= 0) & (me[axis] + offset < size[axis])

    loads = [pltpu.make_async_copy(state_hbm.at[c], st.at[c], in_sem.at[c]) for c in range(5)]
    loads.append(pltpu.make_async_copy(links_hbm, links_ref, in_sem.at[5]))
    loads.append(pltpu.make_async_copy(send_hbm, send_ref, in_sem.at[6]))
    barrier = pltpu.get_barrier_semaphore()
    neighbours = 0
    for place in range(10):
        neighbours = neighbours + exists(place).astype(jnp.int32)

        @pl.when(exists(place))
        def _(place=place):
            pl.semaphore_signal(barrier, inc=1, device_id=device(place), device_id_type=pl.DeviceIdType.MESH)


    for load in loads[::-1]:
        load.start()

    def remote(phase, place):
        src, dst = (send1, recv1) if phase == 0 else (send2, recv2)
        return pltpu.make_async_remote_copy(
            src_ref=src.at[place],
            dst_ref=dst.at[MIRROR[place]],
            send_sem=send_sem.at[phase, place],
            recv_sem=recv_sem.at[phase, MIRROR[place]],
            device_id=device(place),
            device_id_type=pl.DeviceIdType.MESH,
        )

    def start(phase, place):
        @pl.when(exists(place))
        def _():
            remote(phase, place).start()

    def wait_recv(phase, place):
        @pl.when(exists(place))
        def _():
            remote(phase, MIRROR[place]).wait_recv()

    def wait_send(phase, place):
        @pl.when(exists(place))
        def _():
            remote(phase, place).wait_send()

    loads[6].wait()
    loads[5].wait()
    lane = iota(1)
    group = lane >> 5
    slot = lane & 31
    place_of = [
        jnp.where(group < 2, 2 * group + 1, 2 * group),
        jnp.where(group < 2, 2 * group, 2 * group + 1),
        8 + (group & 1),
    ]
    table = send_ref[...]
    t0, t1 = wide(table[:, 0:128]), wide(table[:, 128:256])
    t2 = wide(jnp.concatenate([table[:, 256:320], table[:, 256:320]], axis=1))
    send_index = []
    for k in range(2):
        at = (place_of[k] & 3) * 32 + slot
        send_index.append(jnp.where(group < 2, lane_gather(t0, at), lane_gather(t1, at)) & 127)
    send_index.append(t2 & 127)

    partner = [wide(links_ref[0, k : k + 1, :]) for k in range(3)]
    source = [wide(links_ref[1, k : k + 1, :]) for k in range(3)]
    turns = [wide(links_ref[2, k : k + 1, :]) for k in range(3)]

    def received_index(k, value):
        q = value - 384
        if k == 2:
            first = 1 - ((q >> 5) - 8)
        else:
            first = 3 - (q >> 6)
        return [(((first + j) & 3) * 32 + (q & 31)) for j in range(4)]

    return_index = []
    for k in range(3):
        column = jnp.broadcast_to(jnp.transpose(partner[k])[:, 0:1], (LANES, LANES))
        code = jnp.broadcast_to((384 + place_of[k] * 32 + slot)[0:1, :], (LANES, LANES))
        number = lax.broadcasted_iota(jnp.int32, (LANES, LANES), 0).astype(jnp.float32)
        found = jnp.sum(jnp.where(column == code, number, 0.0), axis=0, keepdims=True)
        return_index.append(wide(found.astype(jnp.int32)))

    def pack(k, get, index, buffer):
        rolled = [index] + [pltpu.roll(index, 32 * j, 1) for j in range(1, 4)]
        for r in range(10):
            u = [lane_gather(get(4 * r + j), rolled[j]) for j in range(4)]
            for b, place in enumerate(PLACES[k]):
                buffer[place, r * 8 : r * 8 + 8, :] = select_groups(group, [((b + j) % 4, u[j]) for j in range(4)])

    def unpack(k, r, buffer):
        v = [buffer[place, r * 8 : r * 8 + 8, :] for place in PLACES[k]]
        last = len(v) - 1
        return [select_groups(group, [((last - b + j) % 4, v[b]) for b in range(len(v))]) for j in range(4)]

    for c in range(5):
        loads[c].wait()
    for k in range(3):
        for c in range(5):
            for a in range(NP):
                low[k, c, a * 8 : a * 8 + 8, :] = st[c, face_rows(k, a, 0), :]
        pack(k, lambda n: low[k, n // 8, (n % 8) * 8 : (n % 8) * 8 + 8, :], send_index[k], send1)

    pl.semaphore_wait(barrier, neighbours)
    order = [0, 7, 1, 6, 2, 5, 3, 4, 8, 9]
    for place in order:
        start(0, place)

    def prim_body(t, carry):
        rows = pl.ds(pl.multiple_of(t * 8, 8), 8)
        u = [st[c, rows, :] for c in range(5)]
        v, p, theta = primitive(u)
        for a in range(3):
            prim[a, rows, :] = v[a]
        prim[3, rows, :] = theta
        return carry

    lax.fori_loop(0, 64, prim_body, 0, unroll=4)

    grad_rows = roll_table(GRAD_MAT)

    def grad_body(s, carry):
        for a in range(4):
            xs = [prim[a, tile(i, s), :] for i in range(NP)]
            for i, y in enumerate(pencil(GRAD_MAT, xs)):
                grad[a, tile(i, s), :] = y
            xs = [prim[a, tile(s, j), :] for j in range(NP)]
            for j, y in enumerate(pencil(GRAD_MAT, xs)):
                grad[4 + a, tile(s, j), :] = y
            for j in range(NP):
                grad[8 + a, tile(s, j), :] = along_rows(grad_rows, xs[j])
        return carry

    lax.fori_loop(0, NP, grad_body, 0)

    for k in (2, 1, 0):
        for place in PLACES[k]:
            wait_recv(0, place)
        index = received_index(k, partner[k])
        own = partner[k] & 127
        local = partner[k] < 384
        for r in range(10):
            u = unpack(k, r, recv1)
            for j in range(4):
                n = 4 * r + j
                rows = slice((n % 8) * 8, (n % 8) * 8 + 8)
                pre[n // 8, rows, :] = jnp.where(
                    local, lane_gather(low[k, n // 8, rows, :], own), lane_gather(u[j], index[j])
                )
        for c in range(5):
            def keep(a, value, k=k, c=c):
                sl[k, c, a * 8 : a * 8 + 8, :] = value
            orient(lambda rows: pre[c, rows, :], keep, turns[k], False)

        def slave_body(a, carry, k=k):
            rows, at = grid_rows(a), face_rows(k, a, 7)
            s = [sl[k, c, rows, :] for c in range(5)]
            u = [st[c, at, :] for c in range(5)]
            vs, ps, ths = primitive(s)
            v = [prim[c, at, :] for c in range(3)]
            th = prim[3, at, :]
            p = th * u[0]
            for c in range(4):
                jump = (vs + [ths])[c] - (v + [th])[c]
                grad[4 * k + c, at, :] = grad[4 * k + c, at, :] + LIFT * jump
            speed = jnp.maximum(jnp.abs(v[k]) + jnp.sqrt(GAMMA * th), jnp.abs(vs[k]) + jnp.sqrt(GAMMA * ths))
            weight = 0.5 * speed + PENALTY
            e = [u[1 + k]] + [u[1 + j] * v[k] for j in range(3)] + [(u[4] + p) * v[k]]
            es = [s[1 + k]] + [s[1 + j] * vs[k] for j in range(3)] + [(s[4] + ps) * vs[k]]
            e[1 + k] = e[1 + k] + p
            es[1 + k] = es[1 + k] + ps
            for c in range(5):
                mf[k, c, rows, :] = 0.5 * (e[c] + es[c]) + weight * (u[c] - s[c])
            return carry

        lax.fori_loop(0, NP, slave_body, 0, unroll=8)

    def stress_heat(k, at, v):
        g = [[grad[4 * d + c, at, :] for c in range(3)] for d in range(3)]
        div = (2.0 / 3.0) * (g[0][0] + g[1][1] + g[2][2])
        stress = [g[k][j] + g[j][k] for j in range(3)]
        stress[k] = stress[k] - div
        heat = stress[0] * v[0] + stress[1] * v[1] + stress[2] * v[2]
        return stress, heat + (CONDUCTION / VISCOSITY) * grad[4 * k + 3, at, :]

    for k in (1, 0, 2):
        def viscous_body(a, carry, k=k):
            rows, at = grid_rows(a), face_rows(k, a, 7)
            v = [prim[c, at, :] for c in range(3)]
            stress, heat = stress_heat(k, at, v)
            for j in range(3):
                mf[k, 1 + j, rows, :] = mf[k, 1 + j, rows, :] - stress[j]
            mf[k, 4, rows, :] = mf[k, 4, rows, :] - heat
            return carry

        lax.fori_loop(0, NP, viscous_body, 0, unroll=8)
        for c in range(5):
            def keep(a, value, k=k, c=c):
                sf[k, c, a * 8 : a * 8 + 8, :] = value
            orient(lambda rows: mf[k, c, rows, :], keep, turns[k], True)
        pack(k, lambda n: sf[k, n // 8, (n % 8) * 8 : (n % 8) * 8 + 8, :], return_index[k], send2)
        for place in PLACES[k]:
            start(1, place)

    def flux_body(t, carry):
        rows = pl.ds(pl.multiple_of(t * 8, 8), 8)
        u = [st[c, rows, :] for c in range(5)]
        v = [prim[c, rows, :] for c in range(3)]
        p = prim[3, rows, :] * u[0]
        g = [[grad[4 * d + c, rows, :] for c in range(4)] for d in range(3)]
        div = (2.0 / 3.0) * (g[0][0] + g[1][1] + g[2][2])
        stress = {}
        number = 0
        for a in range(3):
            for b in range(a, 3):
                stress[a, b] = stress[b, a] = g[a][b] + g[b][a] if a != b else 2.0 * g[a][a] - div
                total = u[1 + a] * v[b] - stress[a, b]
                flux[number, rows, :] = total + p if a == b else total
                number += 1
        enthalpy = u[4] + p
        for k in range(3):
            heat = stress[k, 0] * v[0] + stress[k, 1] * v[1] + stress[k, 2] * v[2]
            heat = heat + (CONDUCTION / VISCOSITY) * g[k][3]
            flux[6 + k, rows, :] = enthalpy * v[k] - heat
        return carry

    lax.fori_loop(0, 64, flux_body, 0, unroll=2)

    flux_rows = roll_table(FLUX_MAT)
    pairs = {(0, 0): 0, (0, 1): 1, (0, 2): 2, (1, 1): 3, (1, 2): 4, (2, 2): 5}

    def flux_of(k, c, rows):
        if c == 0:
            return st[1 + k, rows, :]
        if c == 4:
            return flux[6 + k, rows, :]
        return flux[pairs[min(k, c - 1), max(k, c - 1)], rows, :]

    def first_body(s, carry):
        for c in range(5):
            xs = [flux_of(0, c, tile(i, s)) for i in range(NP)]
            for i, y in enumerate(pencil(FLUX_MAT, xs)):
                upd[c, tile(i, s), :] = y
        return carry

    lax.fori_loop(0, NP, first_body, 0)

    def other_body(s, carry):
        for c in range(5):
            ys = pencil(FLUX_MAT, [flux_of(1, c, tile(s, j)) for j in range(NP)])
            for j in range(NP):
                rows = tile(s, j)
                upd[c, rows, :] = upd[c, rows, :] + ys[j] + along_rows(flux_rows, flux_of(2, c, rows))
        return carry

    lax.fori_loop(0, NP, other_body, 0)

    for k in range(3):
        for c in range(5):
            for a in range(NP):
                at = face_rows(k, a, 7)
                upd[c, at, :] = upd[c, at, :] - FACE_SCALE * mf[k, c, a * 8 : a * 8 + 8, :]

    for k in (2, 1, 0):
        for place in PLACES[k]:
            wait_recv(1, place)
        index = received_index(k, source[k])
        own = source[k] & 127
        local = source[k] < 384
        for r in range(10):
            u = unpack(k, r, recv2)
            for j in range(4):
                n = 4 * r + j
                c, a = n // 8, n % 8
                value = jnp.where(
                    local, lane_gather(sf[k, c, a * 8 : a * 8 + 8, :], own), lane_gather(u[j], index[j])
                )
                at = face_rows(k, a, 0)
                upd[c, at, :] = upd[c, at, :] + FACE_SCALE * value

    for phase in range(2):
        for place in order:
            wait_send(phase, place)


def writer(upd, st, upd_out, sec_out, sec, sem):
    copies = []
    for c in range(5):
        copies.append(pltpu.make_async_copy(upd.at[c], upd_out.at[c], sem.at[0, c]))
        copies[-1].start()
    for c in range(5):
        sec[c] = st[c] + SECTION_WEIGHT * upd[c]
        copies.append(pltpu.make_async_copy(sec.at[c], sec_out.at[c], sem.at[1, c]))
        copies[-1].start()
    for copy in copies:
        copy.wait()


def per_device(n_dom, n_sub, state, face_links, send_from):
    whole = pltpu.VMEM
    f32 = jnp.float32
    field = (512, LANES)
    hbm = pl.BlockSpec(memory_space=pltpu.HBM)
    inside = pl.BlockSpec(memory_space=whole)
    like = jax.ShapeDtypeStruct(state.shape, f32)
    state, face_links, send_from = [
        pltpu.with_memory_space_constraint(x, pltpu.HBM) for x in (state, face_links, send_from)
    ]
    upd, st = pl.pallas_call(
        functools.partial(kernel, n_dom, n_sub),
        out_shape=(like, like),
        in_specs=[hbm, hbm, hbm],
        out_specs=(inside, inside),
        scratch_shapes=[
            whole(face_links.shape, jnp.int32),
            whole(send_from.shape, jnp.int32),
            whole((4,) + field, f32),
            whole((12,) + field, f32),
            whole((9,) + field, f32),
            whole((3, 5, 64, LANES), f32),
            whole((5, 64, LANES), f32),
            whole((3, 5, 64, LANES), f32),
            whole((3, 5, 64, LANES), f32),
            whole((3, 5, 64, LANES), f32),
            whole((10, 80, LANES), f32),
            whole((10, 80, LANES), f32),
            whole((10, 80, LANES), f32),
            whole((10, 80, LANES), f32),
            pltpu.SemaphoreType.DMA((7,)),
            pltpu.SemaphoreType.DMA((2, 10)),
            pltpu.SemaphoreType.DMA((2, 10)),
        ],
        compiler_params=pltpu.CompilerParams(
            collective_id=0, has_side_effects=True, vmem_limit_bytes=40 * 1024 * 1024
        ),
        name="rate",
    )(state, face_links, send_from)
    return pl.pallas_call(
        writer,
        out_shape=(like, like),
        in_specs=[inside, inside],
        out_specs=(hbm, hbm),
        scratch_shapes=[whole((5,) + field, f32), pltpu.SemaphoreType.DMA((2, 5))],
        compiler_params=pltpu.CompilerParams(vmem_limit_bytes=16 * 1024 * 1024),
        name="section",
    )(upd, st)


def solution(mesh):
    in_specs = (
        P(None, None, ("dom", "sub")),
        P(None, None, ("dom", "sub")),
        P(("dom", "sub"), None),
    )
    out_specs = (P(None, None, ("dom", "sub")), P(None, None, ("dom", "sub")))
    return jax.shard_map(
        functools.partial(per_device, mesh.shape["dom"], mesh.shape["sub"]),
        mesh=mesh, in_specs=in_specs, out_specs=out_specs, check_vma=False
    )
```

```python
import functools

import jax
import jax.numpy as jnp
import numpy as np
from jax import lax
from jax.experimental import pallas as pl
from jax.experimental.pallas import tpu as pltpu
from jax.sharding import PartitionSpec as P

NP = 8
LANES = 128
GAMMA = 1.4
VISCOSITY = 0.02
CONDUCTION = VISCOSITY * GAMMA / ((GAMMA - 1.0) * 0.72)
PENALTY = 0.4
TIME_STEP = 0.02
SECTION_WEIGHT = 1432997174477.0 / 9575080441755.0
OFFSETS = [("dom", o) for o in (-4, -3, -2, -1, 1, 2, 3, 4)] + [("sub", -1), ("sub", 1)]
MIRROR = [7, 6, 5, 4, 3, 2, 1, 0, 9, 8]
PLACES = [[1, 3, 4, 6], [0, 2, 5, 7], [8, 9]]


def lobatto(points):
    poly_order = points - 1
    abscissa = -np.cos(np.pi * np.arange(points) / poly_order)
    for sweep in range(60):
        before = abscissa * 0.0 + 1.0
        current = abscissa
        for degree in range(2, points):
            before, current = (
                current,
                ((2 * degree - 1) * abscissa * current - (degree - 1) * before) / degree,
            )
        abscissa = abscissa - (abscissa * current - before) / (points * current)
    identity = np.eye(points)
    spacing = abscissa[:, None] - abscissa[None, :] + identity
    barycentric = 1.0 / np.prod(spacing, axis=1)
    matrix = barycentric[None, :] / barycentric[:, None] / spacing * (1.0 - identity)
    matrix = matrix - identity * np.sum(matrix, axis=1)[:, None]
    return (matrix, 2.0 / (poly_order * points))


DMAT, W_END = lobatto(NP)
GRAD_MAT = VISCOSITY * DMAT
LIFT = VISCOSITY / W_END
FLUX_MAT = DMAT.copy()
FLUX_MAT[NP - 1, NP - 1] -= 1.0 / W_END
FLUX_MAT[0, 0] += 1.0 / W_END
FLUX_MAT = -TIME_STEP * FLUX_MAT
FACE_SCALE = TIME_STEP / W_END


def iota(axis):
    return lax.broadcasted_iota(jnp.int32, (NP, LANES), axis)


def lane_gather(x, index):
    return jnp.take_along_axis(x, index, axis=1, mode="promise_in_bounds")


def row_gather(x, index):
    return jnp.take_along_axis(x, index, axis=0, mode="promise_in_bounds")


def pencil(matrix, xs):
    even = [xs[m] + xs[7 - m] for m in range(4)]
    odd = [xs[m] - xs[7 - m] for m in range(4)]
    out = [None] * 8
    for i in range(4):
        a = b = None
        for m in range(4):
            ce = float(0.5 * (matrix[i, m] + matrix[i, 7 - m]))
            co = float(0.5 * (matrix[i, m] - matrix[i, 7 - m]))
            a = ce * even[m] if a is None else a + ce * even[m]
            b = co * odd[m] if b is None else b + co * odd[m]
        out[i] = a + b
        out[7 - i] = b - a
    return out


def roll_table(matrix):
    row = iota(0)
    table = []
    for r in range(NP):
        c = jnp.zeros((NP, LANES), jnp.float32)
        for l in range(NP):
            c = jnp.where(row == l, float(matrix[l, (l - r) % NP]), c)
        table.append(c)
    return table


def along_rows(table, x):
    acc = table[0] * x
    for r in range(1, NP):
        acc = acc + table[r] * pltpu.roll(x, r, 0)
    return acc


def tile(i, j):
    return pl.ds(pl.multiple_of(i * 64 + j * 8, 8), 8)


def face_rows(k, a, end):
    if k == 0:
        return pl.ds(pl.multiple_of(end * 64 + a * 8, 8), 8)
    if k == 1:
        return pl.ds(pl.multiple_of(a * 64 + end * 8, 8), 8)
    return pl.ds(a * 64 + end, 8, stride=8)


def grid_rows(a):
    return pl.ds(pl.multiple_of(a * 8, 8), 8)


def wide(row):
    return jnp.broadcast_to(row, (NP, LANES))


def select_groups(group, pieces):
    out = pieces[-1][1]
    for g, value in pieces[:-1]:
        out = jnp.where(group == g, value, out)
    return out


def primitive(u):
    inv = 1.0 / u[0]
    v = [u[1] * inv, u[2] * inv, u[3] * inv]
    p = (GAMMA - 1.0) * (u[4] - 0.5 * (u[1] * v[0] + u[2] * v[1] + u[3] * v[2]))
    return v, p, p * inv


def orient(load, store, turns, back):
    m = [load(grid_rows(a)) for a in range(NP)]
    t = [load(pl.ds(a, 8, stride=8)) for a in range(NP)]
    row = iota(0)
    one, three = (3, 1) if back else (1, 3)
    kept = (turns == 0) | (turns == one)
    index = jnp.where(kept, row, 7 - row)
    for a in range(NP):
        x = jnp.where(turns == 0, m[a], jnp.where(turns == one, t[7 - a], jnp.where(turns == 2, m[7 - a], t[a])))
        store(a, row_gather(x, index))


def kernel(n_dom, n_sub, state_hbm, links_hbm, send_hbm, upd, st,
           links_ref, send_ref, prim, grad, flux, low, pre, sl, mf, sf, send1, recv1, send2, recv2,
           in_sem, send_sem, recv_sem):
    me = {"dom": lax.axis_index("dom"), "sub": lax.axis_index("sub")}
    size = {"dom": n_dom, "sub": n_sub}

    def device(place):
        axis, offset = OFFSETS[place]
        at = dict(me)
        at[axis] = me[axis] + offset
        return (at["dom"], at["sub"])

    def exists(place):
        axis, offset = OFFSETS[place]
        return (me[axis] + offset >= 0) & (me[axis] + offset < size[axis])

    loads = [pltpu.make_async_copy(state_hbm.at[c], st.at[c], in_sem.at[c]) for c in range(5)]
    loads.append(pltpu.make_async_copy(links_hbm, links_ref, in_sem.at[5]))
    loads.append(pltpu.make_async_copy(send_hbm, send_ref, in_sem.at[6]))
    barrier = pltpu.get_barrier_semaphore()
    neighbours = 0
    for place in range(10):
        neighbours = neighbours + exists(place).astype(jnp.int32)

        @pl.when(exists(place))
        def _(place=place):
            pl.semaphore_signal(barrier, inc=1, device_id=device(place), device_id_type=pl.DeviceIdType.MESH)


    for load in loads[::-1]:
        load.start()

    def remote(phase, place):
        src, dst = (send1, recv1) if phase == 0 else (send2, recv2)
        return pltpu.make_async_remote_copy(
            src_ref=src.at[place],
            dst_ref=dst.at[MIRROR[place]],
            send_sem=send_sem.at[phase, place],
            recv_sem=recv_sem.at[phase, MIRROR[place]],
            device_id=device(place),
            device_id_type=pl.DeviceIdType.MESH,
        )

    def arriving(phase, place):
        src, dst = (send1, recv1) if phase == 0 else (send2, recv2)
        return pltpu.make_async_remote_copy(
            src_ref=src.at[place],
            dst_ref=dst.at[place],
            send_sem=send_sem.at[phase, place],
            recv_sem=recv_sem.at[phase, place],
            device_id=device(place),
            device_id_type=pl.DeviceIdType.MESH,
        )

    def start(phase, place):
        @pl.when(exists(place))
        def _():
            remote(phase, place).start()

    def wait_recv(phase, place):
        @pl.when(exists(place))
        def _():
            arriving(phase, place).wait_recv()

    def wait_send(phase, place):
        @pl.when(exists(place))
        def _():
            remote(phase, place).wait_send()

    loads[6].wait()
    loads[5].wait()
    lane = iota(1)
    group = lane >> 5
    slot = lane & 31
    place_of = [
        jnp.where(group < 2, 2 * group + 1, 2 * group),
        jnp.where(group < 2, 2 * group, 2 * group + 1),
        8 + (group & 1),
    ]
    table = send_ref[...]
    t0, t1 = wide(table[:, 0:128]), wide(table[:, 128:256])
    t2 = wide(jnp.concatenate([table[:, 256:320], table[:, 256:320]], axis=1))
    send_index = []
    for k in range(2):
        at = (place_of[k] & 3) * 32 + slot
        send_index.append(jnp.where(group < 2, lane_gather(t0, at), lane_gather(t1, at)) & 127)
    send_index.append(t2 & 127)

    partner = [wide(links_ref[0, k : k + 1, :]) for k in range(3)]
    source = [wide(links_ref[1, k : k + 1, :]) for k in range(3)]
    turns = [wide(links_ref[2, k : k + 1, :]) for k in range(3)]

    def received_index(k, value):
        q = value - 384
        if k == 2:
            first = 1 - ((q >> 5) - 8)
        else:
            first = 3 - (q >> 6)
        return [(((first + j) & 3) * 32 + (q & 31)) for j in range(4)]

    return_index = []
    for k in range(3):
        column = jnp.broadcast_to(jnp.transpose(partner[k])[:, 0:1], (LANES, LANES))
        code = jnp.broadcast_to((384 + place_of[k] * 32 + slot)[0:1, :], (LANES, LANES))
        number = lax.broadcasted_iota(jnp.int32, (LANES, LANES), 0).astype(jnp.float32)
        found = jnp.sum(jnp.where(column == code, number, 0.0), axis=0, keepdims=True)
        return_index.append(wide(found.astype(jnp.int32)))

    def pack(k, get, index, buffer):
        rolled = [index] + [pltpu.roll(index, 32 * j, 1) for j in range(1, 4)]
        for r in range(10):
            u = [lane_gather(get(4 * r + j), rolled[j]) for j in range(4)]
            for b, place in enumerate(PLACES[k]):
                buffer[place, r * 8 : r * 8 + 8, :] = select_groups(group, [((b + j) % 4, u[j]) for j in range(4)])

    def unpack(k, r, buffer):
        v = [buffer[place, r * 8 : r * 8 + 8, :] for place in PLACES[k]]
        last = len(v) - 1
        return [select_groups(group, [((last - b + j) % 4, v[b]) for b in range(len(v))]) for j in range(4)]

    for c in range(5):
        loads[c].wait()
    for k in range(3):
        for c in range(5):
            for a in range(NP):
                low[k, c, a * 8 : a * 8 + 8, :] = st[c, face_rows(k, a, 0), :]
        pack(k, lambda n: low[k, n // 8, (n % 8) * 8 : (n % 8) * 8 + 8, :], send_index[k], send1)

    pl.semaphore_wait(barrier, neighbours)
    order = [0, 7, 1, 6, 2, 5, 3, 4, 8, 9]
    for place in order:
        start(0, place)

    def prim_body(t, carry):
        rows = pl.ds(pl.multiple_of(t * 8, 8), 8)
        u = [st[c, rows, :] for c in range(5)]
        v, p, theta = primitive(u)
        for a in range(3):
            prim[a, rows, :] = v[a]
        prim[3, rows, :] = theta
        return carry

    lax.fori_loop(0, 64, prim_body, 0, unroll=4)

    grad_rows = roll_table(GRAD_MAT)

    def grad_body(s, carry):
        for a in range(4):
            xs = [prim[a, tile(i, s), :] for i in range(NP)]
            for i, y in enumerate(pencil(GRAD_MAT, xs)):
                grad[a, tile(i, s), :] = y
            xs = [prim[a, tile(s, j), :] for j in range(NP)]
            for j, y in enumerate(pencil(GRAD_MAT, xs)):
                grad[4 + a, tile(s, j), :] = y
            for j in range(NP):
                grad[8 + a, tile(s, j), :] = along_rows(grad_rows, xs[j])
        return carry

    lax.fori_loop(0, NP, grad_body, 0)

    for k in (2, 1, 0):
        for place in PLACES[k]:
            wait_recv(0, place)
        index = received_index(k, partner[k])
        own = partner[k] & 127
        local = partner[k] < 384
        for r in range(10):
            u = unpack(k, r, recv1)
            for j in range(4):
                n = 4 * r + j
                rows = slice((n % 8) * 8, (n % 8) * 8 + 8)
                pre[n // 8, rows, :] = jnp.where(
                    local, lane_gather(low[k, n // 8, rows, :], own), lane_gather(u[j], index[j])
                )
        for c in range(5):
            def keep(a, value, k=k, c=c):
                sl[k, c, a * 8 : a * 8 + 8, :] = value
            orient(lambda rows: pre[c, rows, :], keep, turns[k], False)

        def slave_body(a, carry, k=k):
            rows, at = grid_rows(a), face_rows(k, a, 7)
            s = [sl[k, c, rows, :] for c in range(5)]
            u = [st[c, at, :] for c in range(5)]
            vs, ps, ths = primitive(s)
            v = [prim[c, at, :] for c in range(3)]
            th = prim[3, at, :]
            p = th * u[0]
            for c in range(4):
                jump = (vs + [ths])[c] - (v + [th])[c]
                grad[4 * k + c, at, :] = grad[4 * k + c, at, :] + LIFT * jump
            speed = jnp.maximum(jnp.abs(v[k]) + jnp.sqrt(GAMMA * th), jnp.abs(vs[k]) + jnp.sqrt(GAMMA * ths))
            weight = 0.5 * speed + PENALTY
            e = [u[1 + k]] + [u[1 + j] * v[k] for j in range(3)] + [(u[4] + p) * v[k]]
            es = [s[1 + k]] + [s[1 + j] * vs[k] for j in range(3)] + [(s[4] + ps) * vs[k]]
            e[1 + k] = e[1 + k] + p
            es[1 + k] = es[1 + k] + ps
            for c in range(5):
                mf[k, c, rows, :] = 0.5 * (e[c] + es[c]) + weight * (u[c] - s[c])
            return carry

        lax.fori_loop(0, NP, slave_body, 0, unroll=8)

    def stress_heat(k, at, v):
        g = [[grad[4 * d + c, at, :] for c in range(3)] for d in range(3)]
        div = (2.0 / 3.0) * (g[0][0] + g[1][1] + g[2][2])
        stress = [g[k][j] + g[j][k] for j in range(3)]
        stress[k] = stress[k] - div
        heat = stress[0] * v[0] + stress[1] * v[1] + stress[2] * v[2]
        return stress, heat + (CONDUCTION / VISCOSITY) * grad[4 * k + 3, at, :]

    for k in (1, 0, 2):
        def viscous_body(a, carry, k=k):
            rows, at = grid_rows(a), face_rows(k, a, 7)
            v = [prim[c, at, :] for c in range(3)]
            stress, heat = stress_heat(k, at, v)
            for j in range(3):
                mf[k, 1 + j, rows, :] = mf[k, 1 + j, rows, :] - stress[j]
            mf[k, 4, rows, :] = mf[k, 4, rows, :] - heat
            return carry

        lax.fori_loop(0, NP, viscous_body, 0, unroll=8)
        for c in range(5):
            def keep(a, value, k=k, c=c):
                sf[k, c, a * 8 : a * 8 + 8, :] = value
            orient(lambda rows: mf[k, c, rows, :], keep, turns[k], True)
        pack(k, lambda n: sf[k, n // 8, (n % 8) * 8 : (n % 8) * 8 + 8, :], return_index[k], send2)
        for place in PLACES[k]:
            start(1, place)

    def flux_body(t, carry):
        rows = pl.ds(pl.multiple_of(t * 8, 8), 8)
        u = [st[c, rows, :] for c in range(5)]
        v = [prim[c, rows, :] for c in range(3)]
        p = prim[3, rows, :] * u[0]
        g = [[grad[4 * d + c, rows, :] for c in range(4)] for d in range(3)]
        div = (2.0 / 3.0) * (g[0][0] + g[1][1] + g[2][2])
        stress = {}
        number = 0
        for a in range(3):
            for b in range(a, 3):
                stress[a, b] = stress[b, a] = g[a][b] + g[b][a] if a != b else 2.0 * g[a][a] - div
                total = u[1 + a] * v[b] - stress[a, b]
                flux[number, rows, :] = total + p if a == b else total
                number += 1
        enthalpy = u[4] + p
        for k in range(3):
            heat = stress[k, 0] * v[0] + stress[k, 1] * v[1] + stress[k, 2] * v[2]
            heat = heat + (CONDUCTION / VISCOSITY) * g[k][3]
            flux[6 + k, rows, :] = enthalpy * v[k] - heat
        return carry

    lax.fori_loop(0, 64, flux_body, 0, unroll=2)

    flux_rows = roll_table(FLUX_MAT)
    pairs = {(0, 0): 0, (0, 1): 1, (0, 2): 2, (1, 1): 3, (1, 2): 4, (2, 2): 5}

    def flux_of(k, c, rows):
        if c == 0:
            return st[1 + k, rows, :]
        if c == 4:
            return flux[6 + k, rows, :]
        return flux[pairs[min(k, c - 1), max(k, c - 1)], rows, :]

    def first_body(s, carry):
        for c in range(5):
            xs = [flux_of(0, c, tile(i, s)) for i in range(NP)]
            for i, y in enumerate(pencil(FLUX_MAT, xs)):
                upd[c, tile(i, s), :] = y
        return carry

    lax.fori_loop(0, NP, first_body, 0)

    def other_body(s, carry):
        for c in range(5):
            ys = pencil(FLUX_MAT, [flux_of(1, c, tile(s, j)) for j in range(NP)])
            for j in range(NP):
                rows = tile(s, j)
                upd[c, rows, :] = upd[c, rows, :] + ys[j] + along_rows(flux_rows, flux_of(2, c, rows))
        return carry

    lax.fori_loop(0, NP, other_body, 0)

    for k in range(3):
        for c in range(5):
            for a in range(NP):
                at = face_rows(k, a, 7)
                upd[c, at, :] = upd[c, at, :] - FACE_SCALE * mf[k, c, a * 8 : a * 8 + 8, :]

    for k in (2, 1, 0):
        for place in PLACES[k]:
            wait_recv(1, place)
        index = received_index(k, source[k])
        own = source[k] & 127
        local = source[k] < 384
        for r in range(10):
            u = unpack(k, r, recv2)
            for j in range(4):
                n = 4 * r + j
                c, a = n // 8, n % 8
                value = jnp.where(
                    local, lane_gather(sf[k, c, a * 8 : a * 8 + 8, :], own), lane_gather(u[j], index[j])
                )
                at = face_rows(k, a, 0)
                upd[c, at, :] = upd[c, at, :] + FACE_SCALE * value

    for phase in range(2):
        for place in order:
            wait_send(phase, place)


def writer(upd, st, upd_out, sec_out, sec, sem):
    copies = []
    for c in range(5):
        copies.append(pltpu.make_async_copy(upd.at[c], upd_out.at[c], sem.at[0, c]))
        copies[-1].start()
    for c in range(5):
        sec[c] = st[c] + SECTION_WEIGHT * upd[c]
        copies.append(pltpu.make_async_copy(sec.at[c], sec_out.at[c], sem.at[1, c]))
        copies[-1].start()
    for copy in copies:
        copy.wait()


def per_device(n_dom, n_sub, state, face_links, send_from):
    whole = pltpu.VMEM
    f32 = jnp.float32
    field = (512, LANES)
    hbm = pl.BlockSpec(memory_space=pltpu.HBM)
    inside = pl.BlockSpec(memory_space=whole)
    like = jax.ShapeDtypeStruct(state.shape, f32)
    state, face_links, send_from = [
        pltpu.with_memory_space_constraint(x, pltpu.HBM) for x in (state, face_links, send_from)
    ]
    upd, st = pl.pallas_call(
        functools.partial(kernel, n_dom, n_sub),
        out_shape=(like, like),
        in_specs=[hbm, hbm, hbm],
        out_specs=(inside, inside),
        scratch_shapes=[
            whole(face_links.shape, jnp.int32),
            whole(send_from.shape, jnp.int32),
            whole((4,) + field, f32),
            whole((12,) + field, f32),
            whole((9,) + field, f32),
            whole((3, 5, 64, LANES), f32),
            whole((5, 64, LANES), f32),
            whole((3, 5, 64, LANES), f32),
            whole((3, 5, 64, LANES), f32),
            whole((3, 5, 64, LANES), f32),
            whole((10, 80, LANES), f32),
            whole((10, 80, LANES), f32),
            whole((10, 80, LANES), f32),
            whole((10, 80, LANES), f32),
            pltpu.SemaphoreType.DMA((7,)),
            pltpu.SemaphoreType.DMA((2, 10)),
            pltpu.SemaphoreType.DMA((2, 10)),
        ],
        compiler_params=pltpu.CompilerParams(
            collective_id=0, has_side_effects=True, vmem_limit_bytes=40 * 1024 * 1024
        ),
        name="rate",
    )(state, face_links, send_from)
    return pl.pallas_call(
        writer,
        out_shape=(like, like),
        in_specs=[inside, inside],
        out_specs=(hbm, hbm),
        scratch_shapes=[whole((5,) + field, f32), pltpu.SemaphoreType.DMA((2, 5))],
        compiler_params=pltpu.CompilerParams(vmem_limit_bytes=16 * 1024 * 1024),
        name="section",
    )(upd, st)


def solution(mesh):
    in_specs = (
        P(None, None, ("dom", "sub")),
        P(None, None, ("dom", "sub")),
        P(("dom", "sub"), None),
    )
    out_specs = (P(None, None, ("dom", "sub")), P(None, None, ("dom", "sub")))
    return jax.shard_map(
        functools.partial(per_device, mesh.shape["dom"], mesh.shape["sub"]),
        mesh=mesh, in_specs=in_specs, out_specs=out_specs, check_vma=False
    )
```

```python
import functools

import jax
import jax.numpy as jnp
import numpy as np
from jax import lax
from jax.experimental import pallas as pl
from jax.experimental.pallas import tpu as pltpu
from jax.sharding import PartitionSpec as P

NP = 8
LANES = 128
GAMMA = 1.4
VISCOSITY = 0.02
CONDUCTION = VISCOSITY * GAMMA / ((GAMMA - 1.0) * 0.72)
PENALTY = 0.4
TIME_STEP = 0.02
SECTION_WEIGHT = 1432997174477.0 / 9575080441755.0
OFFSETS = [("dom", o) for o in (-4, -3, -2, -1, 1, 2, 3, 4)] + [("sub", -1), ("sub", 1)]
MIRROR = [7, 6, 5, 4, 3, 2, 1, 0, 9, 8]
PLACES = [[1, 3, 4, 6], [0, 2, 5, 7], [8, 9]]
SENDS = [[1, 6, 3, 4], [0, 7, 2, 5], [8, 9]]


def lobatto(points):
    poly_order = points - 1
    abscissa = -np.cos(np.pi * np.arange(points) / poly_order)
    for sweep in range(60):
        before = abscissa * 0.0 + 1.0
        current = abscissa
        for degree in range(2, points):
            before, current = (
                current,
                ((2 * degree - 1) * abscissa * current - (degree - 1) * before) / degree,
            )
        abscissa = abscissa - (abscissa * current - before) / (points * current)
    identity = np.eye(points)
    spacing = abscissa[:, None] - abscissa[None, :] + identity
    barycentric = 1.0 / np.prod(spacing, axis=1)
    matrix = barycentric[None, :] / barycentric[:, None] / spacing * (1.0 - identity)
    matrix = matrix - identity * np.sum(matrix, axis=1)[:, None]
    return (matrix, 2.0 / (poly_order * points))


DMAT, W_END = lobatto(NP)
GRAD_MAT = VISCOSITY * DMAT
LIFT = VISCOSITY / W_END
FLUX_MAT = DMAT.copy()
FLUX_MAT[NP - 1, NP - 1] -= 1.0 / W_END
FLUX_MAT[0, 0] += 1.0 / W_END
FLUX_MAT = -TIME_STEP * FLUX_MAT
FACE_SCALE = TIME_STEP / W_END


def iota(axis):
    return lax.broadcasted_iota(jnp.int32, (NP, LANES), axis)


def lane_gather(x, index):
    return jnp.take_along_axis(x, index, axis=1, mode="promise_in_bounds")


def row_gather(x, index):
    return jnp.take_along_axis(x, index, axis=0, mode="promise_in_bounds")


def pencil(matrix, xs):
    even = [xs[m] + xs[7 - m] for m in range(4)]
    odd = [xs[m] - xs[7 - m] for m in range(4)]
    out = [None] * 8
    for i in range(4):
        a = b = None
        for m in range(4):
            ce = float(0.5 * (matrix[i, m] + matrix[i, 7 - m]))
            co = float(0.5 * (matrix[i, m] - matrix[i, 7 - m]))
            a = ce * even[m] if a is None else a + ce * even[m]
            b = co * odd[m] if b is None else b + co * odd[m]
        out[i] = a + b
        out[7 - i] = b - a
    return out


def roll_table(matrix):
    row = iota(0)
    table = []
    for r in range(NP):
        c = jnp.zeros((NP, LANES), jnp.float32)
        for l in range(NP):
            c = jnp.where(row == l, float(matrix[l, (l - r) % NP]), c)
        table.append(c)
    return table


def along_rows(table, x):
    acc = table[0] * x
    for r in range(1, NP):
        acc = acc + table[r] * pltpu.roll(x, r, 0)
    return acc


def tile(i, j):
    return pl.ds(pl.multiple_of(i * 64 + j * 8, 8), 8)


def face_rows(k, a, end):
    if k == 0:
        return pl.ds(pl.multiple_of(end * 64 + a * 8, 8), 8)
    if k == 1:
        return pl.ds(pl.multiple_of(a * 64 + end * 8, 8), 8)
    return pl.ds(a * 64 + end, 8, stride=8)


def grid_rows(a):
    return pl.ds(pl.multiple_of(a * 8, 8), 8)


def wide(row):
    return jnp.broadcast_to(row, (NP, LANES))


def select_groups(group, pieces):
    out = pieces[-1][1]
    for g, value in pieces[:-1]:
        out = jnp.where(group == g, value, out)
    return out


def primitive(u):
    inv = 1.0 / u[0]
    v = [u[1] * inv, u[2] * inv, u[3] * inv]
    p = (GAMMA - 1.0) * (u[4] - 0.5 * (u[1] * v[0] + u[2] * v[1] + u[3] * v[2]))
    return v, p, p * inv


def orient(load, store, turns, back):
    m = [load(grid_rows(a)) for a in range(NP)]
    t = [load(pl.ds(a, 8, stride=8)) for a in range(NP)]
    row = iota(0)
    one, three = (3, 1) if back else (1, 3)
    kept = (turns == 0) | (turns == one)
    index = jnp.where(kept, row, 7 - row)
    for a in range(NP):
        x = jnp.where(turns == 0, m[a], jnp.where(turns == one, t[7 - a], jnp.where(turns == 2, m[7 - a], t[a])))
        store(a, row_gather(x, index))


def kernel(n_dom, n_sub, state_hbm, links_hbm, send_hbm, upd, st,
           links_ref, send_ref, prim, grad, flux, low, pre, sl, mf, sf, send1, recv1, send2, recv2,
           in_sem, send_sem, recv_sem):
    me = {"dom": lax.axis_index("dom"), "sub": lax.axis_index("sub")}
    size = {"dom": n_dom, "sub": n_sub}

    def device(place):
        axis, offset = OFFSETS[place]
        at = dict(me)
        at[axis] = me[axis] + offset
        return (at["dom"], at["sub"])

    def exists(place):
        axis, offset = OFFSETS[place]
        return (me[axis] + offset >= 0) & (me[axis] + offset < size[axis])

    loads = [pltpu.make_async_copy(state_hbm.at[c], st.at[c], in_sem.at[c]) for c in range(5)]
    loads.append(pltpu.make_async_copy(links_hbm, links_ref, in_sem.at[5]))
    loads.append(pltpu.make_async_copy(send_hbm, send_ref, in_sem.at[6]))
    barrier = pltpu.get_barrier_semaphore()
    neighbours = 0
    for place in range(10):
        neighbours = neighbours + exists(place).astype(jnp.int32)

        @pl.when(exists(place))
        def _(place=place):
            pl.semaphore_signal(barrier, inc=1, device_id=device(place), device_id_type=pl.DeviceIdType.MESH)


    for load in loads[::-1]:
        load.start()

    def remote(phase, place):
        src, dst = (send1, recv1) if phase == 0 else (send2, recv2)
        return pltpu.make_async_remote_copy(
            src_ref=src.at[place],
            dst_ref=dst.at[MIRROR[place]],
            send_sem=send_sem.at[phase, place],
            recv_sem=recv_sem.at[phase, MIRROR[place]],
            device_id=device(place),
            device_id_type=pl.DeviceIdType.MESH,
        )

    def arriving(phase, place):
        src, dst = (send1, recv1) if phase == 0 else (send2, recv2)
        return pltpu.make_async_remote_copy(
            src_ref=src.at[place],
            dst_ref=dst.at[place],
            send_sem=send_sem.at[phase, place],
            recv_sem=recv_sem.at[phase, place],
            device_id=device(place),
            device_id_type=pl.DeviceIdType.MESH,
        )

    def start(phase, place):
        @pl.when(exists(place))
        def _():
            remote(phase, place).start()

    def wait_recv(phase, place):
        @pl.when(exists(place))
        def _():
            arriving(phase, place).wait_recv()

    def wait_send(phase, place):
        @pl.when(exists(place))
        def _():
            remote(phase, place).wait_send()

    loads[6].wait()
    loads[5].wait()
    lane = iota(1)
    group = lane >> 5
    slot = lane & 31
    place_of = [
        jnp.where(group < 2, 2 * group + 1, 2 * group),
        jnp.where(group < 2, 2 * group, 2 * group + 1),
        8 + (group & 1),
    ]
    table = send_ref[...]
    t0, t1 = wide(table[:, 0:128]), wide(table[:, 128:256])
    t2 = wide(jnp.concatenate([table[:, 256:320], table[:, 256:320]], axis=1))
    send_index = []
    for k in range(2):
        at = (place_of[k] & 3) * 32 + slot
        send_index.append(jnp.where(group < 2, lane_gather(t0, at), lane_gather(t1, at)) & 127)
    send_index.append(t2 & 127)

    partner = [wide(links_ref[0, k : k + 1, :]) for k in range(3)]
    source = [wide(links_ref[1, k : k + 1, :]) for k in range(3)]
    turns = [wide(links_ref[2, k : k + 1, :]) for k in range(3)]

    def received_index(k, value):
        q = value - 384
        if k == 2:
            first = 1 - ((q >> 5) - 8)
        else:
            first = 3 - (q >> 6)
        return [(((first + j) & 3) * 32 + (q & 31)) for j in range(4)]

    return_index = []
    for k in range(3):
        column = jnp.broadcast_to(jnp.transpose(partner[k])[:, 0:1], (LANES, LANES))
        code = jnp.broadcast_to((384 + place_of[k] * 32 + slot)[0:1, :], (LANES, LANES))
        number = lax.broadcasted_iota(jnp.int32, (LANES, LANES), 0).astype(jnp.float32)
        found = jnp.sum(jnp.where(column == code, number, 0.0), axis=0, keepdims=True)
        return_index.append(wide(found.astype(jnp.int32)))

    def pack(k, get, index, buffer):
        rolled = [index] + [pltpu.roll(index, 32 * j, 1) for j in range(1, 4)]
        for r in range(10):
            u = [lane_gather(get(4 * r + j), rolled[j]) for j in range(4)]
            for b, place in enumerate(PLACES[k]):
                buffer[place, r * 8 : r * 8 + 8, :] = select_groups(group, [((b + j) % 4, u[j]) for j in range(4)])

    def unpack(k, r, buffer):
        v = [buffer[place, r * 8 : r * 8 + 8, :] for place in PLACES[k]]
        last = len(v) - 1
        return [select_groups(group, [((last - b + j) % 4, v[b]) for b in range(len(v))]) for j in range(4)]

    for c in range(5):
        loads[c].wait()
    for k in range(3):
        for c in range(5):
            for a in range(NP):
                low[k, c, a * 8 : a * 8 + 8, :] = st[c, face_rows(k, a, 0), :]
        pack(k, lambda n: low[k, n // 8, (n % 8) * 8 : (n % 8) * 8 + 8, :], send_index[k], send1)

    pl.semaphore_wait(barrier, neighbours)
    order = [0, 7, 1, 6, 2, 5, 3, 4, 8, 9]
    for place in order:
        start(0, place)

    def prim_body(t, carry):
        rows = pl.ds(pl.multiple_of(t * 8, 8), 8)
        u = [st[c, rows, :] for c in range(5)]
        v, p, theta = primitive(u)
        for a in range(3):
            prim[a, rows, :] = v[a]
        prim[3, rows, :] = theta
        return carry

    lax.fori_loop(0, 64, prim_body, 0, unroll=4)

    grad_rows = roll_table(GRAD_MAT)

    def grad_body(s, carry):
        for a in range(4):
            xs = [prim[a, tile(i, s), :] for i in range(NP)]
            for i, y in enumerate(pencil(GRAD_MAT, xs)):
                grad[a, tile(i, s), :] = y
            xs = [prim[a, tile(s, j), :] for j in range(NP)]
            for j, y in enumerate(pencil(GRAD_MAT, xs)):
                grad[4 + a, tile(s, j), :] = y
            for j in range(NP):
                grad[8 + a, tile(s, j), :] = along_rows(grad_rows, xs[j])
        return carry

    lax.fori_loop(0, NP, grad_body, 0)

    for k in (2, 1, 0):
        for place in PLACES[k]:
            wait_recv(0, place)
        index = received_index(k, partner[k])
        own = partner[k] & 127
        local = partner[k] < 384
        for r in range(10):
            u = unpack(k, r, recv1)
            for j in range(4):
                n = 4 * r + j
                rows = slice((n % 8) * 8, (n % 8) * 8 + 8)
                pre[n // 8, rows, :] = jnp.where(
                    local, lane_gather(low[k, n // 8, rows, :], own), lane_gather(u[j], index[j])
                )
        for c in range(5):
            def keep(a, value, k=k, c=c):
                sl[k, c, a * 8 : a * 8 + 8, :] = value
            orient(lambda rows: pre[c, rows, :], keep, turns[k], False)

        def slave_body(a, carry, k=k):
            rows, at = grid_rows(a), face_rows(k, a, 7)
            s = [sl[k, c, rows, :] for c in range(5)]
            u = [st[c, at, :] for c in range(5)]
            vs, ps, ths = primitive(s)
            v = [prim[c, at, :] for c in range(3)]
            th = prim[3, at, :]
            p = th * u[0]
            for c in range(4):
                jump = (vs + [ths])[c] - (v + [th])[c]
                grad[4 * k + c, at, :] = grad[4 * k + c, at, :] + LIFT * jump
            speed = jnp.maximum(jnp.abs(v[k]) + jnp.sqrt(GAMMA * th), jnp.abs(vs[k]) + jnp.sqrt(GAMMA * ths))
            weight = 0.5 * speed + PENALTY
            e = [u[1 + k]] + [u[1 + j] * v[k] for j in range(3)] + [(u[4] + p) * v[k]]
            es = [s[1 + k]] + [s[1 + j] * vs[k] for j in range(3)] + [(s[4] + ps) * vs[k]]
            e[1 + k] = e[1 + k] + p
            es[1 + k] = es[1 + k] + ps
            for c in range(5):
                mf[k, c, rows, :] = 0.5 * (e[c] + es[c]) + weight * (u[c] - s[c])
            return carry

        lax.fori_loop(0, NP, slave_body, 0, unroll=8)

    def stress_heat(k, at, v):
        g = [[grad[4 * d + c, at, :] for c in range(3)] for d in range(3)]
        div = (2.0 / 3.0) * (g[0][0] + g[1][1] + g[2][2])
        stress = [g[k][j] + g[j][k] for j in range(3)]
        stress[k] = stress[k] - div
        heat = stress[0] * v[0] + stress[1] * v[1] + stress[2] * v[2]
        return stress, heat + (CONDUCTION / VISCOSITY) * grad[4 * k + 3, at, :]

    for k in (1, 0, 2):
        def viscous_body(a, carry, k=k):
            rows, at = grid_rows(a), face_rows(k, a, 7)
            v = [prim[c, at, :] for c in range(3)]
            stress, heat = stress_heat(k, at, v)
            for j in range(3):
                mf[k, 1 + j, rows, :] = mf[k, 1 + j, rows, :] - stress[j]
            mf[k, 4, rows, :] = mf[k, 4, rows, :] - heat
            return carry

        lax.fori_loop(0, NP, viscous_body, 0, unroll=8)
        for c in range(5):
            def keep(a, value, k=k, c=c):
                sf[k, c, a * 8 : a * 8 + 8, :] = value
            orient(lambda rows: mf[k, c, rows, :], keep, turns[k], True)
        pack(k, lambda n: sf[k, n // 8, (n % 8) * 8 : (n % 8) * 8 + 8, :], return_index[k], send2)
        for place in SENDS[k]:
            start(1, place)

    def flux_body(t, carry):
        rows = pl.ds(pl.multiple_of(t * 8, 8), 8)
        u = [st[c, rows, :] for c in range(5)]
        v = [prim[c, rows, :] for c in range(3)]
        p = prim[3, rows, :] * u[0]
        g = [[grad[4 * d + c, rows, :] for c in range(4)] for d in range(3)]
        div = (2.0 / 3.0) * (g[0][0] + g[1][1] + g[2][2])
        stress = {}
        number = 0
        for a in range(3):
            for b in range(a, 3):
                stress[a, b] = stress[b, a] = g[a][b] + g[b][a] if a != b else 2.0 * g[a][a] - div
                total = u[1 + a] * v[b] - stress[a, b]
                flux[number, rows, :] = total + p if a == b else total
                number += 1
        enthalpy = u[4] + p
        for k in range(3):
            heat = stress[k, 0] * v[0] + stress[k, 1] * v[1] + stress[k, 2] * v[2]
            heat = heat + (CONDUCTION / VISCOSITY) * g[k][3]
            flux[6 + k, rows, :] = enthalpy * v[k] - heat
        return carry

    lax.fori_loop(0, 64, flux_body, 0, unroll=2)

    flux_rows = roll_table(FLUX_MAT)
    pairs = {(0, 0): 0, (0, 1): 1, (0, 2): 2, (1, 1): 3, (1, 2): 4, (2, 2): 5}

    def flux_of(k, c, rows):
        if c == 0:
            return st[1 + k, rows, :]
        if c == 4:
            return flux[6 + k, rows, :]
        return flux[pairs[min(k, c - 1), max(k, c - 1)], rows, :]

    def first_body(s, carry):
        for c in range(5):
            xs = [flux_of(0, c, tile(i, s)) for i in range(NP)]
            for i, y in enumerate(pencil(FLUX_MAT, xs)):
                upd[c, tile(i, s), :] = y
        return carry

    lax.fori_loop(0, NP, first_body, 0)

    def other_body(s, carry):
        for c in range(5):
            ys = pencil(FLUX_MAT, [flux_of(1, c, tile(s, j)) for j in range(NP)])
            for j in range(NP):
                rows = tile(s, j)
                upd[c, rows, :] = upd[c, rows, :] + ys[j] + along_rows(flux_rows, flux_of(2, c, rows))
        return carry

    lax.fori_loop(0, NP, other_body, 0)

    for k in range(3):
        for c in range(5):
            for a in range(NP):
                at = face_rows(k, a, 7)
                upd[c, at, :] = upd[c, at, :] - FACE_SCALE * mf[k, c, a * 8 : a * 8 + 8, :]

    for k in (2, 1, 0):
        for place in PLACES[k]:
            wait_recv(1, place)
        index = received_index(k, source[k])
        own = source[k] & 127
        local = source[k] < 384
        for r in range(10):
            u = unpack(k, r, recv2)
            for j in range(4):
                n = 4 * r + j
                c, a = n // 8, n % 8
                value = jnp.where(
                    local, lane_gather(sf[k, c, a * 8 : a * 8 + 8, :], own), lane_gather(u[j], index[j])
                )
                at = face_rows(k, a, 0)
                upd[c, at, :] = upd[c, at, :] + FACE_SCALE * value

    for phase in range(2):
        for place in order:
            wait_send(phase, place)


def writer(upd, st, upd_out, sec_out, sec, sem):
    copies = []
    for c in range(5):
        copies.append(pltpu.make_async_copy(upd.at[c], upd_out.at[c], sem.at[0, c]))
        copies[-1].start()
    for c in range(5):
        sec[c] = st[c] + SECTION_WEIGHT * upd[c]
        copies.append(pltpu.make_async_copy(sec.at[c], sec_out.at[c], sem.at[1, c]))
        copies[-1].start()
    for copy in copies:
        copy.wait()


def per_device(n_dom, n_sub, state, face_links, send_from):
    whole = pltpu.VMEM
    f32 = jnp.float32
    field = (512, LANES)
    hbm = pl.BlockSpec(memory_space=pltpu.HBM)
    inside = pl.BlockSpec(memory_space=whole)
    like = jax.ShapeDtypeStruct(state.shape, f32)
    state, face_links, send_from = [
        pltpu.with_memory_space_constraint(x, pltpu.HBM) for x in (state, face_links, send_from)
    ]
    upd, st = pl.pallas_call(
        functools.partial(kernel, n_dom, n_sub),
        out_shape=(like, like),
        in_specs=[hbm, hbm, hbm],
        out_specs=(inside, inside),
        scratch_shapes=[
            whole(face_links.shape, jnp.int32),
            whole(send_from.shape, jnp.int32),
            whole((4,) + field, f32),
            whole((12,) + field, f32),
            whole((9,) + field, f32),
            whole((3, 5, 64, LANES), f32),
            whole((5, 64, LANES), f32),
            whole((3, 5, 64, LANES), f32),
            whole((3, 5, 64, LANES), f32),
            whole((3, 5, 64, LANES), f32),
            whole((10, 80, LANES), f32),
            whole((10, 80, LANES), f32),
            whole((10, 80, LANES), f32),
            whole((10, 80, LANES), f32),
            pltpu.SemaphoreType.DMA((7,)),
            pltpu.SemaphoreType.DMA((2, 10)),
            pltpu.SemaphoreType.DMA((2, 10)),
        ],
        compiler_params=pltpu.CompilerParams(
            collective_id=0, has_side_effects=True, vmem_limit_bytes=40 * 1024 * 1024
        ),
        name="rate",
    )(state, face_links, send_from)
    return pl.pallas_call(
        writer,
        out_shape=(like, like),
        in_specs=[inside, inside],
        out_specs=(hbm, hbm),
        scratch_shapes=[whole((5,) + field, f32), pltpu.SemaphoreType.DMA((2, 5))],
        compiler_params=pltpu.CompilerParams(vmem_limit_bytes=16 * 1024 * 1024),
        name="section",
    )(upd, st)


def solution(mesh):
    in_specs = (
        P(None, None, ("dom", "sub")),
        P(None, None, ("dom", "sub")),
        P(("dom", "sub"), None),
    )
    out_specs = (P(None, None, ("dom", "sub")), P(None, None, ("dom", "sub")))
    return jax.shard_map(
        functools.partial(per_device, mesh.shape["dom"], mesh.shape["sub"]),
        mesh=mesh, in_specs=in_specs, out_specs=out_specs, check_vma=False
    )
```
